32 devices in a mesh: pairs: 2 (over x), tgt: 16 (over z, y, core).
Axes of the slice: x: 2, y: 2, z: 4, core: 2. Of those that a mesh axis runs over, the one named last changes fastest.
Arguments:
- source_features: bfloat16 [256, 1024], P(('pairs', 'tgt')), parts along dimension 0, may hold values from -6 to 6
- target_features: bfloat16 [64, 128, 1024], P(('pairs', 'tgt')), parts along dimension 0, may hold values from -6 to 6
- conv_first: float32 [16, 3, 3, 3, 3], replicated, may hold values from -2 to 2
- conv_second: float32 [16, 3, 3, 3, 3], replicated, may hold values from -0.625 to 0.625
Outputs:
- filtered: float32 [2, 128, 32, 128], P('pairs', None, 'tgt'), parts along dimension 0
The draws below stay inside these ranges and needn't reach their ends.
There are 2 independent parts, one for each index of `pairs`. The reference program is written for one: setup_inputs(seed, part) draws one part's arguments, and reference() takes and returns one part's arrays. A program takes and returns all parts, laid end to end along the dimension named above; an argument that names none is the same for every part. Nothing has to cross between parts.
All inputs are finite; a program needn't handle non-finite values.
Results may differ from the reference program's by a relative error of at most 0.0028.
Values may be sent and summed in bfloat16 or wider, within the bound.
A program may use at most 128 MiB of HBM per device.

```python
import math
from functools import reduce
import jax
import jax.numpy as jnp
from jax import lax

C = 1024
HID = 16
SR = 1
WA = 128
WB = 128
RB_DEV = 2
SA = 128
HB = 32
N_TGT = 16


pattern_count = 64


def pattern_table(key):
    channel_picks = jax.random.randint(jax.random.fold_in(key, 11), (pattern_count, C), 0, 8)
    return (channel_picks < 3).astype(jnp.float32)


def cell_support(key, row_count, pattern_rows):
    pattern_ids = jax.random.randint(jax.random.fold_in(key, 1), (row_count,), 0, pattern_count)
    kept_mask = (jax.random.randint(jax.random.fold_in(key, 2), (row_count, C), 0, 10) < 7).astype(jnp.float32)
    return pattern_rows[pattern_ids] * kept_mask


def cell_levels(key, row_count):
    levels = jax.random.uniform(key, (row_count, C), jnp.float32, 0.05, 1.0)
    return levels


def assemble(key, support, levels):
    row_count = support.shape[0]
    scales = jnp.exp(jax.random.uniform(jax.random.fold_in(key, 1), (row_count, 1), jnp.float32, math.log(0.6), math.log(6.0)))
    jitter_field = 0.15 * jax.random.normal(jax.random.fold_in(key, 2), (row_count, C), jnp.float32)
    background = -0.5 + jitter_field
    values = scales * (support * levels + (1.0 - support) * background)
    return jnp.clip(values, -6.0, 6.0)


def source_parts(key):
    pattern_rows = pattern_table(key)
    support = cell_support(jax.random.fold_in(key, 21), SA, pattern_rows)
    levels = cell_levels(jax.random.fold_in(key, 22), SA)
    return (support, levels)


def draw_source_features(key, part):
    support, levels = source_parts(key)
    values = assemble(jax.random.fold_in(key, 23), support, levels)
    return values.astype(jnp.bfloat16)


def draw_target_features(key, part):
    pattern_rows = pattern_table(key)
    cell_count = HB * WB
    support = cell_support(jax.random.fold_in(key, 31), cell_count, pattern_rows)
    levels = cell_levels(jax.random.fold_in(key, 32), cell_count)
    source_support, source_levels = source_parts(key)
    chosen = jax.random.permutation(jax.random.fold_in(key, 33), cell_count)[:SA].astype(jnp.int32)
    jitter = 0.03 * jax.random.normal(jax.random.fold_in(key, 34), (SA, C), jnp.float32)
    matched = jnp.clip(source_levels + jitter, 0.01, 1.0)
    support = support.at[chosen].set(source_support)
    levels = levels.at[chosen].set(matched)
    values = assemble(jax.random.fold_in(key, 35), support, levels)
    return values.reshape(HB, WB, C).astype(jnp.bfloat16)


def gaussian(stream_key, dims, deviation, most, kind=jnp.bfloat16):
    array = jax.random.normal(stream_key, dims, jnp.float32) * deviation
    return jnp.minimum(jnp.maximum(array, -most), most).astype(kind)


def setup_inputs(seed: int = 0, part: int = 0) -> dict:
    key_list = jax.random.split(jax.random.key(seed), 5)
    part_keys = jax.random.split(jax.random.fold_in(key_list[4], part), 5)
    source_features = draw_source_features(jax.random.fold_in(jax.random.fold_in(key_list[4], part), 71), part)
    target_features = draw_target_features(jax.random.fold_in(jax.random.fold_in(key_list[4], part), 71), part)
    conv_first = gaussian(key_list[2], (HID, 3, 3, 3, 3), 9 ** -0.5, 2.0, jnp.float32)
    conv_second = gaussian(key_list[3], (HID, 3, 3, 3, 3), 81 ** -0.5, 0.625, jnp.float32)
    return dict(source_features=source_features, target_features=target_features, conv_first=conv_first, conv_second=conv_second)


EPSILON = 1e-05

def normalize(features):
    positive = jax.nn.relu(features.astype(jnp.float32))
    length = jnp.sqrt(lax.optimization_barrier(jnp.sum(positive * positive, axis=-1, keepdims=True)) + 1e-06)
    return (positive / length).astype(jnp.bfloat16)

def mutual_filter(volume, target_best):
    source_best = lax.optimization_barrier(jnp.max(volume, axis=(0, 1), keepdims=True))
    return volume * (volume / (source_best + EPSILON)) * (volume / (target_best[:, :, None, None] + EPSILON))

def offsets_used(source_rows):
    picks = []
    for first in range(3):
        if abs(first - 1) < source_rows:
            for second in range(3):
                for third in range(3):
                    for fourth in range(3):
                        picks.append((first, second, third, fourth))
    return picks

def layer_one(volume, kernel):
    src_rows, src_cols, rows_in, tgt_cols = volume.shape
    rows_out = rows_in - 2
    padded = jnp.pad(volume, ((1, 1), (1, 1), (0, 0), (1, 1)))
    picks = offsets_used(src_rows)
    stacked = jnp.stack([padded[a:a + src_rows, b:b + src_cols, c:c + rows_out, d:d + tgt_cols] for a, b, c, d in picks]).reshape(len(picks), -1)
    weights = jnp.stack([kernel[:, a, b, c, d] for a, b, c, d in picks], axis=1)
    hidden = jnp.dot(weights, stacked, precision=lax.Precision.HIGHEST, preferred_element_type=jnp.float32)
    return hidden.reshape(kernel.shape[0], src_rows, src_cols, rows_out, tgt_cols)

def layer_two(hidden, kernel):
    channels, src_rows, src_cols, rows_in, tgt_cols = hidden.shape
    rows_out = rows_in - 2
    picks = offsets_used(src_rows)
    weights = jnp.stack([kernel[:, a, b, c, d] for a, b, c, d in picks], axis=0)
    spread = jnp.dot(weights, hidden.reshape(channels, -1), precision=lax.Precision.HIGHEST, preferred_element_type=jnp.float32)
    spread = spread.reshape(len(picks), src_rows, src_cols, rows_in, tgt_cols)
    padded = jnp.pad(spread, ((0, 0), (1, 1), (1, 1), (0, 0), (1, 1)))
    pieces = [padded[number, a:a + src_rows, b:b + src_cols, c:c + rows_out, d:d + tgt_cols] for number, (a, b, c, d) in enumerate(picks)]
    return reduce(lambda left, right: left + right, pieces)

def transpose_kernel(kernel):
    return jnp.transpose(kernel, (0, 3, 4, 1, 2))

def consensus_deep(margin_volume, conv_first, conv_second, inside_grid):
    result = None
    kernel_pairs = ((conv_first, conv_second), (transpose_kernel(conv_first), transpose_kernel(conv_second)))
    for first_kernel, second_kernel in kernel_pairs:
        hidden = jax.nn.relu(layer_one(margin_volume, first_kernel))
        hidden = jnp.where(inside_grid[None, None, None, :, None], hidden, jnp.zeros_like(hidden))
        output = jax.nn.relu(layer_two(hidden, second_kernel))
        result = output if result is None else result + output
    return result

def reference(source_features, target_features, conv_first, conv_second):
    source_unit = normalize(source_features)
    target_unit = normalize(target_features.reshape(HB * WB, C))
    correlation = jnp.dot(source_unit, target_unit.T, preferred_element_type=jnp.float32).reshape(SR, WA, HB, WB)
    target_best = lax.optimization_barrier(jnp.max(correlation, axis=(2, 3)))
    mutual_first = mutual_filter(correlation, target_best)
    padded = jnp.pad(mutual_first, ((0, 0), (0, 0), (2, 2), (0, 0)))

    def one_block(block):
        start_row = (block * RB_DEV).astype(jnp.int32)
        window = lax.dynamic_slice_in_dim(padded, start_row, RB_DEV + 4, axis=2)
        global_rows = start_row - 1 + jnp.arange(RB_DEV + 2, dtype=jnp.int32)
        inside_grid = (global_rows >= 0) & (global_rows < HB)
        return consensus_deep(window, conv_first, conv_second, inside_grid)
    blocks = lax.map(one_block, jnp.arange(N_TGT, dtype=jnp.int32))
    consensus = jnp.transpose(blocks, (1, 2, 0, 3, 4)).reshape(SR, WA, HB, WB)
    final_best = lax.optimization_barrier(jnp.max(consensus, axis=(2, 3)))
    return mutual_filter(consensus, final_best)
```

```python
import functools

import jax
import jax.numpy as jnp
import numpy as np
from jax import lax
from jax.experimental import pallas as pl
from jax.experimental.pallas import tpu as pltpu
from jax.sharding import PartitionSpec as P

EPSILON = 1e-05
MESH = pl.DeviceIdType.MESH
F32 = jnp.float32
BF16 = jnp.bfloat16
STEPS = 4
COLUMN = 64
GROUP = 6


def tap_number(branch, b, c, d):
    return 27 + 9 * b + 3 * c + d if branch == 0 else 27 * c + 9 * d + 3 + b


def first_selector():
    table = np.zeros((2, 256, 256), np.float32)
    for branch in range(2):
        for b in range(3):
            for c in range(3):
                for d in range(3):
                    tap = tap_number(branch, b, c, d)
                    for part in range(3):
                        row = tap + (128 if part == 2 else 0)
                        column = b * COLUMN + part * 3 * GROUP + d * GROUP + c
                        table[branch, row, column] = 1
    return table


def second_selector():
    table = np.zeros((2, 128, 1024), np.float32)
    for branch in range(2):
        for jj in range(2):
            for r in range(4):
                for group in range(2):
                    for d in range(3):
                        for jo in range(2):
                            for k in range(2):
                                b = jj - jo + 2 - 2 * group
                                c = r - k
                                if 0 <= b <= 2 and 0 <= c <= 2:
                                    tap = tap_number(branch, b, c, d)
                                    column = group * 24 + d * 8 + branch * 4 + jo * 2 + k
                                    table[branch, tap, (jj * 4 + r) * 128 + column] = 1
    return table


def unit(features):
    positive = jnp.maximum(features.astype(F32), 0.0)
    total = jnp.sum(positive * positive, axis=-1, keepdims=True)
    return positive * (1.0 / jnp.sqrt(total + 1e-06))


def split(value):
    high = value.astype(BF16)
    low = (value - high.astype(F32)).astype(BF16)
    return high, low


def shift_right(value):
    lanes = lax.broadcasted_iota(jnp.int32, value.shape, 1)
    return jnp.where(lanes >= 1, pltpu.roll(value, 1, 1), 0.0)


def shift_left(value):
    width = value.shape[1]
    lanes = lax.broadcasted_iota(jnp.int32, value.shape, 1)
    return jnp.where(lanes < width - 1, pltpu.roll(value, width - 1, 1), 0.0)


def across(row):
    wide = jnp.broadcast_to(row[:1], (128, 128))
    return jnp.transpose(wide)


def kernel(
    n, rows, cells,
    src_ref, tgt_ref, w_ref, e1_ref, e2_ref, out_ref,
    gathered, target_unit, corr, halo, best_one, best_two, window, volume, cons, w1, w2,
    gather_send, gather_recv, halo_send, halo_recv,
    one_send, one_recv, two_send, two_recv,
):
    pair = lax.axis_index("pairs")
    me = lax.axis_index("tgt")

    def device(index):
        return (pair, index)

    def other(step):
        return lax.rem(me + step, n)

    barrier = pltpu.get_barrier_semaphore()

    def greet(step, carry):
        pl.semaphore_signal(barrier, inc=1, device_id=device(other(step)), device_id_type=MESH)
        return carry

    lax.fori_loop(1, n, greet, 0)

    def spread(buffer, send, recv, step):
        to = other(step)
        return pltpu.make_async_remote_copy(
            src_ref=buffer.at[me], dst_ref=buffer.at[me],
            send_sem=send.at[to], recv_sem=recv.at[me],
            device_id=device(to), device_id_type=MESH,
        )

    def arriving(buffer, send, recv, step):
        source = other(step)
        return pltpu.make_async_remote_copy(
            src_ref=buffer.at[source], dst_ref=buffer.at[source],
            send_sem=send.at[source], recv_sem=recv.at[source],
            device_id=device(source), device_id_type=MESH,
        )

    def start_all(*buffers):
        def body(step, carry):
            spread(*buffers, step).start()
            return carry

        lax.fori_loop(1, n, body, 0)

    def receive_all(*buffers):
        def body(step, carry):
            arriving(*buffers, step).wait_recv()
            return carry

        lax.fori_loop(1, n, body, 0)

    def sent_all(*buffers):
        def body(step, carry):
            spread(*buffers, step).wait_send()
            return carry

        lax.fori_loop(1, n, body, 0)

    gather = (gathered, gather_send, gather_recv)
    one = (best_one, one_send, one_recv)
    two = (best_two, two_send, two_recv)

    half = src_ref.shape[1] // 2
    own = unit(src_ref[...])
    gathered[me] = jnp.concatenate([own[:, :half], own[:, half:]], axis=0).astype(BF16)
    pl.semaphore_wait(barrier, n - 1)
    start_all(*gather)

    target_unit[...] = unit(tgt_ref[...]).astype(BF16)

    first_high, first_low = split(w_ref[0:16, :])
    second_high, second_low = split(w_ref[16:32, :])
    first_parts = jnp.concatenate([first_high, first_low], axis=1)
    base = jnp.concatenate(
        [jnp.dot(first_parts, e1_ref[branch], preferred_element_type=F32) for branch in range(2)],
        axis=0,
    )
    for jj in range(2):
        for r in range(4):
            row = me * 2 - 1 + r
            inside = jnp.where(jnp.logical_and(row >= 0, row < n * 2), 1.0, 0.0).astype(F32)
            shift = jj * COLUMN + r
            moved = pltpu.roll(base, shift, 1) if shift else base
            start = (jj * 4 + r) * 32
            w1[start : start + 32, :] = (moved * inside).astype(BF16)
    second_parts = jnp.concatenate([second_high, second_low], axis=0)
    picked = [
        jnp.dot(second_parts, e2_ref[branch], preferred_element_type=F32) for branch in range(2)
    ]
    for part in range(2):
        blocks = []
        for number in range(8):
            for branch in range(2):
                blocks.append(
                    picked[branch][part * 16 : part * 16 + 16, number * 128 : number * 128 + 128]
                )
        turned = jnp.transpose(jnp.concatenate(blocks, axis=0))
        w2[part * 48 : part * 48 + 48, :] = turned[:48].astype(BF16)

    receive_all(*gather)
    everyone = gathered[...].astype(F32)
    padded_rows = everyone.shape[1] // 2
    source = jnp.concatenate(
        [
            everyone[:, :padded_rows].reshape(n * padded_rows, half),
            everyone[:, padded_rows:].reshape(n * padded_rows, half),
        ],
        axis=1,
    ).astype(BF16)
    if rows != padded_rows:
        wanted = lax.broadcasted_iota(jnp.int32, (cells, n * padded_rows), 0)
        offered = lax.broadcasted_iota(jnp.int32, (cells, n * padded_rows), 1)
        place = (wanted // rows) * padded_rows + wanted % rows
        choice = jnp.where(place == offered, 1.0, 0.0).astype(BF16)
        source = jnp.dot(choice, source, preferred_element_type=F32).astype(BF16)
    corr[...] = lax.dot_general(
        source, target_unit[...], (((1,), (1,)), ((), ())), preferred_element_type=F32
    )

    def halo_up():
        return pltpu.make_async_remote_copy(
            src_ref=corr, dst_ref=halo.at[0], send_sem=halo_send.at[0], recv_sem=halo_recv.at[0],
            device_id=device(lax.rem(me + 1, n)), device_id_type=MESH,
        )

    def halo_down():
        return pltpu.make_async_remote_copy(
            src_ref=corr, dst_ref=halo.at[1], send_sem=halo_send.at[1], recv_sem=halo_recv.at[1],
            device_id=device(lax.rem(me + n - 1, n)), device_id_type=MESH,
        )

    first, last = me == 0, me == n - 1

    @pl.when(jnp.logical_not(last))
    def _():
        halo_up().start()

    @pl.when(jnp.logical_not(first))
    def _():
        halo_down().start()

    local = jnp.maximum(corr[:, :128], corr[:, 128:])
    best_row = jnp.max(jnp.transpose(local), axis=0, keepdims=True)
    best_one[me] = jnp.broadcast_to(best_row, (8, 128))
    start_all(*one)

    @pl.when(first)
    def _():
        halo[0] = jnp.zeros(halo.shape[1:], F32)

    @pl.when(last)
    def _():
        halo[1] = jnp.zeros(halo.shape[1:], F32)

    blank = jnp.zeros((COLUMN, 128), BF16)
    volume[0] = blank
    for extra in range(cells + 1, volume.shape[0]):
        volume[extra] = blank

    receive_all(*one)
    target_scale = 1.0 / (across(jnp.max(best_one[...], axis=0)) + EPSILON)

    def place_row(slab, k):
        source_scale = 1.0 / (jnp.max(slab, axis=0, keepdims=True) + EPSILON)
        window[pl.ds(k, cells, stride=8), :] = (
            slab * (slab * source_scale) * (slab * target_scale)
        )

    place_row(corr[:, :128], 2)
    place_row(corr[:, 128:], 3)

    @pl.when(jnp.logical_not(first))
    def _():
        halo_up().wait_recv()

    @pl.when(jnp.logical_not(last))
    def _():
        halo_down().wait_recv()

    for side in range(2):
        for k in range(2):
            place_row(halo[side, :, k * 128 : k * 128 + 128], side * 4 + k)

    def lay(step, carry):
        for inner in range(8):
            j = step * 8 + inner
            here = window[pl.ds(pl.multiple_of(j * 8, 8), 8), :]
            moved = jnp.concatenate(
                [shift_right(here)[:GROUP], here[:GROUP], shift_left(here)[:GROUP]], axis=0
            )
            high = moved.astype(BF16).astype(F32)
            rest = jnp.zeros((COLUMN - 9 * GROUP, 128), F32)
            volume[j + 1] = jnp.concatenate([high, moved - high, high, rest], axis=0).astype(BF16)
        return carry

    lax.fori_loop(0, cells // 8, lay, 0)

    def finish(parts):
        total = shift_right(parts[0]) + parts[1] + shift_left(parts[2])
        total = jnp.maximum(total, 0.0)
        return total + pltpu.roll(total, 4, 0)

    def layers(step, carry):
        carry = list(carry)
        for inner in range(STEPS):
            q = step * STEPS + inner
            left = volume[pl.ds(q * 4, 4)].reshape(4 * COLUMN, 128)
            right = volume[pl.ds(q * 4 + 2, 4)].reshape(4 * COLUMN, 128)
            stacked = jnp.concatenate([left, right], axis=1)
            hidden = jnp.dot(w1[...], stacked, preferred_element_type=F32)
            high, low = split(jnp.maximum(hidden, 0.0))
            mixed = jnp.dot(w2[...], high, preferred_element_type=F32)
            found = mixed[:48] + mixed[48:]
            found = found + jnp.dot(w2[:48, :], low, preferred_element_type=F32)
            before = [found[8 * d : 8 * d + 8] for d in range(3)]
            behind = [found[24 + 8 * d : 32 + 8 * d] for d in range(3)]
            even = finish([before[d][:, :128] + carry[d] for d in range(3)])
            odd = finish([before[d][:, 128:] + behind[d][:, :128] for d in range(3)])
            carry = [behind[d][:, 128:] for d in range(3)]
            sublanes = lax.broadcasted_iota(jnp.int32, even.shape, 0)
            cons[pl.ds(pl.multiple_of(q * 8, 8), 8), :] = jnp.where(sublanes < 4, even, odd)
        return tuple(carry)

    nothing = jnp.zeros((8, 128), F32)
    carry = lax.fori_loop(0, cells // (4 * STEPS), layers, (nothing,) * 3)
    cons[2 * cells : 2 * cells + 8, :] = finish(list(carry))

    rows_of = [cons[pl.ds(2 + k, cells, stride=2), :] for k in range(2)]
    best_row = jnp.max(jnp.transpose(jnp.maximum(*rows_of)), axis=0, keepdims=True)
    best_two[me] = jnp.broadcast_to(best_row, (8, 128))
    start_all(*two)
    scaled = [
        value * (value * (1.0 / (jnp.max(value, axis=0, keepdims=True) + EPSILON)))
        for value in rows_of
    ]

    sent_all(*gather)
    sent_all(*one)

    @pl.when(jnp.logical_not(last))
    def _():
        halo_up().wait_send()

    @pl.when(jnp.logical_not(first))
    def _():
        halo_down().wait_send()

    receive_all(*two)
    final_scale = 1.0 / (across(jnp.max(best_two[...], axis=0)) + EPSILON)
    for k in range(2):
        out_ref[pl.ds(k, cells, stride=2), :] = scaled[k] * (rows_of[k] * final_scale)
    sent_all(*two)


def shards(source_features, target_features, conv_first, conv_second):
    n = lax.axis_size("tgt")
    rows, channels = source_features.shape
    local_rows, width = target_features.shape[:2]
    cells = rows * n
    hidden = conv_first.shape[0]
    assert local_rows == 2 and width == 128 and cells == 128 and hidden == 16
    padded_rows = -(-rows // 8) * 8
    if padded_rows != rows:
        source_features = jnp.pad(source_features, ((0, padded_rows - rows), (0, 0)))
    weights = jnp.concatenate([conv_first.reshape(hidden, -1), conv_second.reshape(hidden, -1)])
    weights = jnp.pad(weights, ((0, 0), (0, 128 - weights.shape[1])))
    dma = pltpu.SemaphoreType.DMA
    result = pl.pallas_call(
        functools.partial(kernel, n, rows, cells),
        out_shape=jax.ShapeDtypeStruct((cells * local_rows, width), F32),
        in_specs=[pl.BlockSpec(memory_space=pltpu.VMEM)] * 5,
        out_specs=pl.BlockSpec(memory_space=pltpu.VMEM),
        scratch_shapes=[
            pltpu.VMEM((n, 2 * padded_rows, channels // 2), BF16),
            pltpu.VMEM((local_rows * width, channels), BF16),
            pltpu.VMEM((cells, local_rows * width), F32),
            pltpu.VMEM((2, cells, local_rows * width), F32),
            pltpu.VMEM((n, 8, 128), F32),
            pltpu.VMEM((n, 8, 128), F32),
            pltpu.VMEM((cells * 8, width), F32),
            pltpu.VMEM((cells + 2, COLUMN, width), BF16),
            pltpu.VMEM((cells * 2 + 8, width), F32),
            pltpu.VMEM((256, 256), BF16),
            pltpu.VMEM((96, 256), BF16),
            dma((n,)), dma((n,)), dma((2,)), dma((2,)),
            dma((n,)), dma((n,)), dma((n,)), dma((n,)),
        ],
        compiler_params=pltpu.CompilerParams(
            collective_id=0, has_side_effects=True, vmem_limit_bytes=40 * 1024 * 1024
        ),
        cost_estimate=pl.CostEstimate(
            flops=2 * 10**9, bytes_accessed=3 * 10**6, transcendentals=0
        ),
    )(
        source_features,
        target_features.reshape(local_rows * width, channels),
        weights,
        jnp.asarray(first_selector(), BF16),
        jnp.asarray(second_selector(), BF16),
    )
    return result.reshape(1, cells, local_rows, width)


def solution(mesh):
    placed = (P(("pairs", "tgt"), None), P(("pairs", "tgt"), None, None), P(), P())
    return jax.shard_map(
        shards, mesh=mesh, in_specs=placed, out_specs=P("pairs", None, "tgt", None), check_vma=False
    )
```

```python
import functools

import jax
import jax.numpy as jnp
import numpy as np
from jax import lax
from jax.experimental import pallas as pl
from jax.experimental.pallas import tpu as pltpu
from jax.sharding import PartitionSpec as P

EPSILON = 1e-05
MESH = pl.DeviceIdType.MESH
F32 = jnp.float32
BF16 = jnp.bfloat16
STEPS = 4
VMEM_BYTES = 63 * 1024 * 1024
COLUMN = 64
GROUP = 6
SPAN = 24


def place_of(part, d):
    if part < 2:
        return part * SPAN + d * GROUP
    return 3 * GROUP if d == 2 else 2 * SPAN + d * GROUP


def tap_number(branch, b, c, d):
    tap = 27 + 9 * b + 3 * c + d if branch == 0 else 27 * c + 9 * d + 3 + b
    return tap // 3 * 4 + tap % 3


def first_selector():
    table = np.zeros((2, 256, 256), np.float32)
    for branch in range(2):
        for b in range(3):
            for c in range(3):
                for d in range(3):
                    tap = tap_number(branch, b, c, d)
                    for part in range(3):
                        row = tap + (128 if part == 2 else 0)
                        column = b * COLUMN + place_of(part, d) + c
                        table[branch, row, column] = 1
    return table


def second_selector():
    table = np.zeros((2, 128, 1024), np.float32)
    for branch in range(2):
        for jj in range(2):
            for r in range(4):
                for group in range(2):
                    for d in range(3):
                        for jo in range(2):
                            for k in range(2):
                                b = jj - jo + 2 - 2 * group
                                c = r - k
                                if 0 <= b <= 2 and 0 <= c <= 2:
                                    tap = tap_number(branch, b, c, d)
                                    column = group * 24 + d * 8 + branch * 4 + jo * 2 + k
                                    table[branch, tap, (jj * 4 + r) * 128 + column] = 1
    return table


def unit(features):
    positive = jnp.maximum(features.astype(F32), 0.0)
    total = jnp.sum(positive * positive, axis=-1, keepdims=True)
    return positive * (1.0 / jnp.sqrt(total + 1e-06))


def split(value):
    high = value.astype(BF16)
    low = (value - high.astype(F32)).astype(BF16)
    return high, low


def shift_right(value):
    lanes = lax.broadcasted_iota(jnp.int32, value.shape, 1)
    return jnp.where(lanes >= 1, pltpu.roll(value, 1, 1), 0.0)


def shift_left(value):
    width = value.shape[1]
    lanes = lax.broadcasted_iota(jnp.int32, value.shape, 1)
    return jnp.where(lanes < width - 1, pltpu.roll(value, width - 1, 1), 0.0)


def across(row):
    wide = jnp.broadcast_to(row, (128, 128))
    return jnp.transpose(wide)


def kernel(
    n, rows, cells,
    src_hbm, tgt_hbm, first_hbm, second_hbm, e1_hbm, e2_hbm, out_ref,
    src_ref, tgt_ref, first_ref, second_ref, e1_ref, e2_ref, taps,
    gathered, target_unit, corr, halo, best_one, best_two, window, scales, volume, cons, w1, w2,
    local_sem, gather_send, gather_recv, pass_send, halo_send, halo_recv,
    one_send, one_recv, two_send, two_recv,
):
    pair = lax.axis_index("pairs")
    me = lax.axis_index("tgt")

    def device(index):
        return (pair, index)

    def other(step):
        return lax.rem(me + step, n)

    loads = [
        pltpu.make_async_copy(far, near, local_sem.at[number])
        for number, (far, near) in enumerate(
            [
                (src_hbm, src_ref), (tgt_hbm, tgt_ref), (first_hbm, first_ref),
                (second_hbm, second_ref), (e1_hbm, e1_ref), (e2_hbm, e2_ref),
            ]
        )
    ]
    for load in loads:
        load.start()
    barrier = pltpu.get_barrier_semaphore()

    def greet(step, carry):
        pl.semaphore_signal(barrier, inc=1, device_id=device(other(step)), device_id_type=MESH)
        return carry

    lax.fori_loop(1, n, greet, 0)

    def spread(buffer, send, recv, step):
        to = other(step)
        return pltpu.make_async_remote_copy(
            src_ref=buffer.at[me], dst_ref=buffer.at[me],
            send_sem=send.at[to], recv_sem=recv.at[me],
            device_id=device(to), device_id_type=MESH,
        )

    def arriving(buffer, send, recv, step):
        source = other(step)
        return pltpu.make_async_remote_copy(
            src_ref=buffer.at[source], dst_ref=buffer.at[source],
            send_sem=send.at[source], recv_sem=recv.at[source],
            device_id=device(source), device_id_type=MESH,
        )

    def start_all(*buffers):
        def body(step, carry):
            spread(*buffers, step).start()
            return carry

        lax.fori_loop(1, n, body, 0)

    def receive_all(*buffers):
        def body(step, carry):
            arriving(*buffers, step).wait_recv()
            return carry

        lax.fori_loop(1, n, body, 0)

    def sent_all(*buffers):
        def body(step, carry):
            spread(*buffers, step).wait_send()
            return carry

        lax.fori_loop(1, n, body, 0)

    one = (best_one, one_send, one_recv)
    two = (best_two, two_send, two_recv)

    half = src_ref.shape[1] // 2
    loads[0].wait()
    own = unit(src_ref[...])
    gathered[me] = jnp.concatenate([own[:, :half], own[:, half:]], axis=0).astype(BF16)
    pl.semaphore_wait(barrier, n - 1)

    sibling = me + 1 - 2 * lax.rem(me, 2)

    def gather_to(to):
        return pltpu.make_async_remote_copy(
            src_ref=gathered.at[me], dst_ref=gathered.at[me],
            send_sem=gather_send.at[to], recv_sem=gather_recv.at[me],
            device_id=device(to), device_id_type=MESH,
        )

    def pass_on(index):
        return pltpu.make_async_remote_copy(
            src_ref=gathered.at[index], dst_ref=gathered.at[index],
            send_sem=pass_send.at[index], recv_sem=gather_recv.at[index],
            device_id=device(sibling), device_id_type=MESH,
        )

    def gather_start(step, carry):
        gather_to(other(2 * step)).start()
        return carry

    def gather_pass(step, carry):
        index = lax.rem(me + n - 2 * step, n)
        pass_on(index).wait_recv()
        pass_on(index).start()
        return carry

    def gather_end(step, carry):
        pass_on(lax.rem(sibling + n - 2 * step, n)).wait_recv()
        return carry

    def gather_sent(step, carry):
        gather_to(other(2 * step)).wait_send()
        pass_on(lax.rem(me + n - 2 * step, n)).wait_send()
        return carry

    gather_to(sibling).start()
    lax.fori_loop(1, n // 2, gather_start, 0)

    loads[1].wait()
    target_unit[...] = unit(tgt_ref[...]).astype(BF16)

    taps[...] = jnp.zeros(taps.shape, F32)
    for load in loads[2:]:
        load.wait()
    for number, weights in enumerate((first_ref, second_ref)):
        for tap in range(weights.shape[0]):
            taps[number, 4 * tap : 4 * tap + 3, 0:16] = weights[tap]
    first_high, first_low = split(jnp.transpose(taps[0])[:16])
    second_high, second_low = split(jnp.transpose(taps[1])[:16])
    first_parts = jnp.concatenate([first_high, first_low], axis=1)
    base = jnp.concatenate(
        [jnp.dot(first_parts, e1_ref[branch], preferred_element_type=F32) for branch in range(2)],
        axis=0,
    )
    for jj in range(2):
        for r in range(4):
            row = me * 2 - 1 + r
            inside = jnp.where(jnp.logical_and(row >= 0, row < n * 2), 1.0, 0.0).astype(F32)
            shift = jj * COLUMN + r
            moved = pltpu.roll(base, shift, 1) if shift else base
            start = (jj * 4 + r) * 32
            w1[start : start + 32, :] = (moved * inside).astype(BF16)
    second_parts = jnp.concatenate([second_high, second_low], axis=0)
    picked = [
        jnp.dot(second_parts, e2_ref[branch], preferred_element_type=F32) for branch in range(2)
    ]
    for part in range(2):
        blocks = []
        for number in range(8):
            for branch in range(2):
                blocks.append(
                    picked[branch][part * 16 : part * 16 + 16, number * 128 : number * 128 + 128]
                )
        turned = jnp.transpose(jnp.concatenate(blocks, axis=0))
        w2[part * 48 : part * 48 + 48, :] = turned[:48].astype(BF16)

    lax.fori_loop(1, n // 2, gather_pass, 0)
    lax.fori_loop(0, n // 2, gather_end, 0)
    everyone = gathered[...].astype(F32)
    padded_rows = everyone.shape[1] // 2
    source = jnp.concatenate(
        [
            everyone[:, :padded_rows].reshape(n * padded_rows, half),
            everyone[:, padded_rows:].reshape(n * padded_rows, half),
        ],
        axis=1,
    ).astype(BF16)
    if rows != padded_rows:
        wanted = lax.broadcasted_iota(jnp.int32, (cells, n * padded_rows), 0)
        offered = lax.broadcasted_iota(jnp.int32, (cells, n * padded_rows), 1)
        place = (wanted // rows) * padded_rows + wanted % rows
        choice = jnp.where(place == offered, 1.0, 0.0).astype(BF16)
        source = jnp.dot(choice, source, preferred_element_type=F32).astype(BF16)
    corr[...] = lax.dot_general(
        source, target_unit[...], (((1,), (1,)), ((), ())), preferred_element_type=F32
    )

    def halo_up():
        return pltpu.make_async_remote_copy(
            src_ref=corr, dst_ref=halo.at[0], send_sem=halo_send.at[0], recv_sem=halo_recv.at[0],
            device_id=device(lax.rem(me + 1, n)), device_id_type=MESH,
        )

    def halo_down():
        return pltpu.make_async_remote_copy(
            src_ref=corr, dst_ref=halo.at[1], send_sem=halo_send.at[1], recv_sem=halo_recv.at[1],
            device_id=device(lax.rem(me + n - 1, n)), device_id_type=MESH,
        )

    first, last = me == 0, me == n - 1

    @pl.when(jnp.logical_not(last))
    def _():
        halo_up().start()

    @pl.when(jnp.logical_not(first))
    def _():
        halo_down().start()

    local = jnp.maximum(corr[:, :128], corr[:, 128:])
    best_row = jnp.max(jnp.transpose(local), axis=0, keepdims=True)
    best_one[me] = best_row
    start_all(*one)

    @pl.when(first)
    def _():
        halo[0] = jnp.zeros(halo.shape[1:], F32)

    @pl.when(last)
    def _():
        halo[1] = jnp.zeros(halo.shape[1:], F32)

    blank = jnp.zeros((COLUMN, 128), BF16)
    volume[0] = blank
    for extra in range(cells + 1, volume.shape[0]):
        volume[extra] = blank

    def place_row(slab, k):
        source_scale = 1.0 / (jnp.max(slab, axis=0, keepdims=True) + EPSILON)
        cubed = slab * (slab * source_scale) * slab
        after = shift_left(cubed)
        for group, value in enumerate((shift_right(cubed), cubed, after, after)):
            window[pl.ds(group * GROUP + k, cells, stride=SPAN), :] = value

    place_row(corr[:, :128], 2)
    place_row(corr[:, 128:], 3)

    @pl.when(jnp.logical_not(first))
    def _():
        halo_up().wait_recv()

    @pl.when(jnp.logical_not(last))
    def _():
        halo_down().wait_recv()

    for side in range(2):
        for k in range(2):
            place_row(halo[side, :, k * 128 : k * 128 + 128], side * 4 + k)

    receive_all(*one)
    scales[...] = 1.0 / (across(jnp.max(best_one[...], axis=0)) + EPSILON)

    def lay(step, carry):
        for inner in range(8):
            j = step * 8 + inner
            here = window[pl.ds(pl.multiple_of(j * SPAN, 8), SPAN), :] * scales[pl.ds(j, 1), :]
            high = here.astype(BF16).astype(F32)
            volume[j + 1] = jnp.concatenate([high, here - high, high[:16]], axis=0).astype(BF16)
        return carry

    lax.fori_loop(0, cells // 8, lay, 0)

    def finish(parts):
        total = shift_right(parts[0]) + parts[1] + shift_left(parts[2])
        total = jnp.maximum(total, 0.0)
        return total + pltpu.roll(total, 4, 0)

    def layers(step, carry):
        carry = list(carry)
        for inner in range(STEPS):
            q = step * STEPS + inner
            left = volume[pl.ds(q * 4, 4)].reshape(4 * COLUMN, 128)
            right = volume[pl.ds(q * 4 + 2, 4)].reshape(4 * COLUMN, 128)
            stacked = jnp.concatenate([left, right], axis=1)
            hidden = jnp.dot(w1[...], stacked, preferred_element_type=F32)
            high, low = split(jnp.maximum(hidden, 0.0))
            mixed = jnp.dot(w2[...], high, preferred_element_type=F32)
            found = mixed[:48] + mixed[48:]
            found = found + jnp.dot(w2[:48, :], low, preferred_element_type=F32)
            before = [found[8 * d : 8 * d + 8] for d in range(3)]
            behind = [found[24 + 8 * d : 32 + 8 * d] for d in range(3)]
            even = finish([before[d][:, :128] + carry[d] for d in range(3)])
            odd = finish([before[d][:, 128:] + behind[d][:, :128] for d in range(3)])
            carry = [behind[d][:, 128:] for d in range(3)]
            sublanes = lax.broadcasted_iota(jnp.int32, even.shape, 0)
            cons[pl.ds(pl.multiple_of(q * 8, 8), 8), :] = jnp.where(sublanes < 4, even, odd)
        return tuple(carry)

    nothing = jnp.zeros((8, 128), F32)
    carry = lax.fori_loop(0, cells // (4 * STEPS), layers, (nothing,) * 3)
    cons[2 * cells : 2 * cells + 8, :] = finish(list(carry))

    rows_of = [cons[pl.ds(2 + k, cells, stride=2), :] for k in range(2)]
    best_row = jnp.max(jnp.transpose(jnp.maximum(*rows_of)), axis=0, keepdims=True)
    best_two[me] = best_row
    start_all(*two)
    scaled = [
        value * (value * (1.0 / (jnp.max(value, axis=0, keepdims=True) + EPSILON)))
        for value in rows_of
    ]

    gather_to(sibling).wait_send()
    lax.fori_loop(1, n // 2, gather_sent, 0)
    sent_all(*one)

    @pl.when(jnp.logical_not(last))
    def _():
        halo_up().wait_send()

    @pl.when(jnp.logical_not(first))
    def _():
        halo_down().wait_send()

    receive_all(*two)
    final_scale = 1.0 / (across(jnp.max(best_two[...], axis=0)) + EPSILON)
    for k in range(2):
        out_ref[pl.ds(k, cells, stride=2), :] = scaled[k] * (rows_of[k] * final_scale)
    sent_all(*two)


def shards(source_features, target_features, conv_first, conv_second):
    n = lax.axis_size("tgt")
    rows, channels = source_features.shape
    local_rows, width = target_features.shape[:2]
    cells = rows * n
    hidden = conv_first.shape[0]
    assert local_rows == 2 and width == 128 and cells == 128 and hidden == 16
    padded_rows = -(-rows // 8) * 8
    if padded_rows != rows:
        source_features = jnp.pad(source_features, ((0, padded_rows - rows), (0, 0)))
    selectors = (jnp.asarray(first_selector(), BF16), jnp.asarray(second_selector(), BF16))
    operands = (
        source_features,
        target_features.reshape(local_rows * width, channels),
        jnp.transpose(conv_first, (1, 2, 3, 4, 0)).reshape(27, 3, hidden),
        jnp.transpose(conv_second, (1, 2, 3, 4, 0)).reshape(27, 3, hidden),
        *selectors,
    )
    dma = pltpu.SemaphoreType.DMA
    result = pl.pallas_call(
        functools.partial(kernel, n, rows, cells),
        out_shape=jax.ShapeDtypeStruct((cells * local_rows, width), F32),
        in_specs=[pl.BlockSpec(memory_space=pl.ANY)] * len(operands),
        out_specs=pl.BlockSpec(memory_space=pltpu.VMEM),
        scratch_shapes=[
            *[pltpu.VMEM(operand.shape, operand.dtype) for operand in operands],
            pltpu.VMEM((2, 128, 128), F32),
            pltpu.VMEM((n, 2 * padded_rows, channels // 2), BF16),
            pltpu.VMEM((local_rows * width, channels), BF16),
            pltpu.VMEM((cells, local_rows * width), F32),
            pltpu.VMEM((2, cells, local_rows * width), F32),
            pltpu.VMEM((n, 1, 128), F32),
            pltpu.VMEM((n, 1, 128), F32),
            pltpu.VMEM((cells * SPAN, width), F32),
            pltpu.VMEM((cells, 128), F32),
            pltpu.VMEM((cells + 2, COLUMN, width), BF16),
            pltpu.VMEM((cells * 2 + 8, width), F32),
            pltpu.VMEM((256, 256), BF16),
            pltpu.VMEM((96, 256), BF16),
            dma((len(operands),)), dma((n,)), dma((n,)), dma((n,)), dma((2,)), dma((2,)),
            dma((n,)), dma((n,)), dma((n,)), dma((n,)),
        ],
        compiler_params=pltpu.CompilerParams(
            collective_id=0, has_side_effects=True, vmem_limit_bytes=VMEM_BYTES
        ),
        cost_estimate=pl.CostEstimate(
            flops=2 * 10**9, bytes_accessed=3 * 10**6, transcendentals=0
        ),
    )(*operands)
    return result.reshape(1, cells, local_rows, width)


def solution(mesh):
    placed = (P(("pairs", "tgt"), None), P(("pairs", "tgt"), None, None), P(), P())
    return jax.shard_map(
        shards, mesh=mesh, in_specs=placed, out_specs=P("pairs", None, "tgt", None), check_vma=False
    )
```

```python
import functools

import jax
import jax.numpy as jnp
import numpy as np
from jax import lax
from jax.experimental import pallas as pl
from jax.experimental.pallas import tpu as pltpu
from jax.sharding import PartitionSpec as P

EPSILON = 1e-05
MESH = pl.DeviceIdType.MESH
F32 = jnp.float32
BF16 = jnp.bfloat16
STEPS = 2
VMEM_BYTES = 63 * 1024 * 1024
COLUMN = 64
GROUP = 6
SPAN = 24


def place_of(part, d):
    if part < 2:
        return part * SPAN + d * GROUP
    return 3 * GROUP if d == 2 else 2 * SPAN + d * GROUP


def tap_number(branch, b, c, d):
    tap = 27 + 9 * b + 3 * c + d if branch == 0 else 27 * c + 9 * d + 3 + b
    return tap // 3 * 4 + tap % 3


def first_selector():
    table = np.zeros((2, 256, 256), np.float32)
    for branch in range(2):
        for b in range(3):
            for c in range(3):
                for d in range(3):
                    tap = tap_number(branch, b, c, d)
                    for part in range(3):
                        row = tap + (128 if part == 2 else 0)
                        column = b * COLUMN + place_of(part, d) + c
                        table[branch, row, column] = 1
    return table


def second_selector():
    table = np.zeros((2, 128, 1024), np.float32)
    for branch in range(2):
        for jj in range(2):
            for r in range(4):
                for group in range(2):
                    for d in range(3):
                        for jo in range(2):
                            for k in range(2):
                                b = jj - jo + 2 - 2 * group
                                c = r - k
                                if 0 <= b <= 2 and 0 <= c <= 2:
                                    tap = tap_number(branch, b, c, d)
                                    column = group * 24 + d * 8 + branch * 4 + jo * 2 + k
                                    table[branch, tap, (jj * 4 + r) * 128 + column] = 1
    return table


def unit(features):
    positive = jnp.maximum(features.astype(F32), 0.0)
    total = jnp.sum(positive * positive, axis=-1, keepdims=True)
    return positive * (1.0 / jnp.sqrt(total + 1e-06))


def split(value):
    high = value.astype(BF16)
    low = (value - high.astype(F32)).astype(BF16)
    return high, low


def shift_right(value):
    lanes = lax.broadcasted_iota(jnp.int32, value.shape, 1)
    return jnp.where(lanes >= 1, pltpu.roll(value, 1, 1), 0.0)


def shift_left(value):
    width = value.shape[1]
    lanes = lax.broadcasted_iota(jnp.int32, value.shape, 1)
    return jnp.where(lanes < width - 1, pltpu.roll(value, width - 1, 1), 0.0)


def across(row):
    wide = jnp.broadcast_to(row, (128, 128))
    return jnp.transpose(wide)


def kernel(
    n, rows, cells,
    src_hbm, tgt_hbm, first_hbm, second_hbm, e1_hbm, e2_hbm, out_ref,
    src_ref, tgt_ref, first_ref, second_ref, e1_ref, e2_ref, taps,
    gathered, target_unit, corr, halo, best_one, best_two, window, scales, volume, hidden_even, hidden_odd, cons, w1, w2,
    local_sem, gather_send, gather_recv, pass_send, halo_send, halo_recv,
    one_send, one_recv, two_send, two_recv,
):
    pair = lax.axis_index("pairs")
    me = lax.axis_index("tgt")

    def device(index):
        return (pair, index)

    def other(step):
        return lax.rem(me + step, n)

    loads = [
        pltpu.make_async_copy(far, near, local_sem.at[number])
        for number, (far, near) in enumerate(
            [
                (src_hbm, src_ref), (tgt_hbm, tgt_ref), (first_hbm, first_ref),
                (second_hbm, second_ref), (e1_hbm, e1_ref), (e2_hbm, e2_ref),
            ]
        )
    ]
    for load in loads:
        load.start()
    barrier = pltpu.get_barrier_semaphore()

    def greet(step, carry):
        pl.semaphore_signal(barrier, inc=1, device_id=device(other(step)), device_id_type=MESH)
        return carry

    lax.fori_loop(1, n, greet, 0)

    def spread(buffer, send, recv, step):
        to = other(step)
        return pltpu.make_async_remote_copy(
            src_ref=buffer.at[me], dst_ref=buffer.at[me],
            send_sem=send.at[to], recv_sem=recv.at[me],
            device_id=device(to), device_id_type=MESH,
        )

    def arriving(buffer, send, recv, step):
        source = other(step)
        return pltpu.make_async_remote_copy(
            src_ref=buffer.at[source], dst_ref=buffer.at[source],
            send_sem=send.at[source], recv_sem=recv.at[source],
            device_id=device(source), device_id_type=MESH,
        )

    def start_all(*buffers):
        def body(step, carry):
            spread(*buffers, step).start()
            return carry

        lax.fori_loop(1, n, body, 0)

    def receive_all(*buffers):
        def body(step, carry):
            arriving(*buffers, step).wait_recv()
            return carry

        lax.fori_loop(1, n, body, 0)

    def sent_all(*buffers):
        def body(step, carry):
            spread(*buffers, step).wait_send()
            return carry

        lax.fori_loop(1, n, body, 0)

    one = (best_one, one_send, one_recv)
    two = (best_two, two_send, two_recv)

    half = src_ref.shape[1] // 2
    loads[0].wait()
    own = unit(src_ref[...])
    gathered[me] = jnp.concatenate([own[:, :half], own[:, half:]], axis=0).astype(BF16)
    pl.semaphore_wait(barrier, n - 1)

    sibling = me + 1 - 2 * lax.rem(me, 2)

    def gather_to(to):
        return pltpu.make_async_remote_copy(
            src_ref=gathered.at[me], dst_ref=gathered.at[me],
            send_sem=gather_send.at[to], recv_sem=gather_recv.at[me],
            device_id=device(to), device_id_type=MESH,
        )

    def pass_on(index):
        return pltpu.make_async_remote_copy(
            src_ref=gathered.at[index], dst_ref=gathered.at[index],
            send_sem=pass_send.at[index], recv_sem=gather_recv.at[index],
            device_id=device(sibling), device_id_type=MESH,
        )

    def gather_start(step, carry):
        gather_to(other(2 * step)).start()
        return carry

    def gather_pass(step, carry):
        index = lax.rem(me + n - 2 * step, n)
        pass_on(index).wait_recv()
        pass_on(index).start()
        return carry

    def gather_end(step, carry):
        pass_on(lax.rem(sibling + n - 2 * step, n)).wait_recv()
        return carry

    def gather_sent(step, carry):
        gather_to(other(2 * step)).wait_send()
        pass_on(lax.rem(me + n - 2 * step, n)).wait_send()
        return carry

    gather_to(sibling).start()
    lax.fori_loop(1, n // 2, gather_start, 0)

    loads[1].wait()
    target_unit[...] = unit(tgt_ref[...]).astype(BF16)

    taps[...] = jnp.zeros(taps.shape, F32)
    for load in loads[2:]:
        load.wait()
    for number, weights in enumerate((first_ref, second_ref)):
        for tap in range(weights.shape[0]):
            taps[number, 4 * tap : 4 * tap + 3, 0:16] = weights[tap]
    first_high, first_low = split(jnp.transpose(taps[0])[:16])
    second_high, second_low = split(jnp.transpose(taps[1])[:16])
    first_parts = jnp.concatenate([first_high, first_low], axis=1)
    base = jnp.concatenate(
        [jnp.dot(first_parts, e1_ref[branch], preferred_element_type=F32) for branch in range(2)],
        axis=0,
    )
    for jj in range(2):
        for r in range(4):
            row = me * 2 - 1 + r
            inside = jnp.where(jnp.logical_and(row >= 0, row < n * 2), 1.0, 0.0).astype(F32)
            shift = jj * COLUMN + r
            moved = pltpu.roll(base, shift, 1) if shift else base
            start = (jj * 4 + r) * 32
            w1[start : start + 32, :] = (moved * inside).astype(BF16)
    second_parts = jnp.concatenate([second_high, second_low], axis=0)
    picked = [
        jnp.dot(second_parts, e2_ref[branch], preferred_element_type=F32) for branch in range(2)
    ]
    for part in range(2):
        blocks = []
        for number in range(8):
            for branch in range(2):
                blocks.append(
                    picked[branch][part * 16 : part * 16 + 16, number * 128 : number * 128 + 128]
                )
        turned = jnp.transpose(jnp.concatenate(blocks, axis=0))
        w2[part * 48 : part * 48 + 48, :] = turned[:48].astype(BF16)

    lax.fori_loop(1, n // 2, gather_pass, 0)
    lax.fori_loop(0, n // 2, gather_end, 0)
    everyone = gathered[...].astype(F32)
    padded_rows = everyone.shape[1] // 2
    source = jnp.concatenate(
        [
            everyone[:, :padded_rows].reshape(n * padded_rows, half),
            everyone[:, padded_rows:].reshape(n * padded_rows, half),
        ],
        axis=1,
    ).astype(BF16)
    if rows != padded_rows:
        wanted = lax.broadcasted_iota(jnp.int32, (cells, n * padded_rows), 0)
        offered = lax.broadcasted_iota(jnp.int32, (cells, n * padded_rows), 1)
        place = (wanted // rows) * padded_rows + wanted % rows
        choice = jnp.where(place == offered, 1.0, 0.0).astype(BF16)
        source = jnp.dot(choice, source, preferred_element_type=F32).astype(BF16)
    corr[...] = lax.dot_general(
        source, target_unit[...], (((1,), (1,)), ((), ())), preferred_element_type=F32
    )

    def halo_up():
        return pltpu.make_async_remote_copy(
            src_ref=corr, dst_ref=halo.at[0], send_sem=halo_send.at[0], recv_sem=halo_recv.at[0],
            device_id=device(lax.rem(me + 1, n)), device_id_type=MESH,
        )

    def halo_down():
        return pltpu.make_async_remote_copy(
            src_ref=corr, dst_ref=halo.at[1], send_sem=halo_send.at[1], recv_sem=halo_recv.at[1],
            device_id=device(lax.rem(me + n - 1, n)), device_id_type=MESH,
        )

    first, last = me == 0, me == n - 1

    @pl.when(jnp.logical_not(last))
    def _():
        halo_up().start()

    @pl.when(jnp.logical_not(first))
    def _():
        halo_down().start()

    local = jnp.maximum(corr[:, :128], corr[:, 128:])
    best_row = jnp.max(jnp.transpose(local), axis=0, keepdims=True)
    best_one[me] = best_row
    start_all(*one)

    @pl.when(first)
    def _():
        halo[0] = jnp.zeros(halo.shape[1:], F32)

    @pl.when(last)
    def _():
        halo[1] = jnp.zeros(halo.shape[1:], F32)

    blank = jnp.zeros((COLUMN, 128), BF16)
    volume[0] = blank
    for extra in range(cells + 1, volume.shape[0]):
        volume[extra] = blank

    def place_row(slab, k):
        source_scale = 1.0 / (jnp.max(slab, axis=0, keepdims=True) + EPSILON)
        cubed = slab * (slab * source_scale) * slab
        after = shift_left(cubed)
        for group, value in enumerate((shift_right(cubed), cubed, after, after)):
            window[pl.ds(group * GROUP + k, cells, stride=SPAN), :] = value

    place_row(corr[:, :128], 2)
    place_row(corr[:, 128:], 3)

    @pl.when(jnp.logical_not(first))
    def _():
        halo_up().wait_recv()

    @pl.when(jnp.logical_not(last))
    def _():
        halo_down().wait_recv()

    for side in range(2):
        for k in range(2):
            place_row(halo[side, :, k * 128 : k * 128 + 128], side * 4 + k)

    receive_all(*one)
    scales[...] = 1.0 / (across(jnp.max(best_one[...], axis=0)) + EPSILON)

    def lay(step, carry):
        for inner in range(8):
            j = step * 8 + inner
            here = window[pl.ds(pl.multiple_of(j * SPAN, 8), SPAN), :] * scales[pl.ds(j, 1), :]
            high = here.astype(BF16).astype(F32)
            volume[j + 1] = jnp.concatenate([high, here - high, high[:16]], axis=0).astype(BF16)
        return carry

    lax.fori_loop(0, cells // 8, lay, 0)

    def finish(parts):
        total = shift_right(parts[0]) + parts[1] + shift_left(parts[2])
        total = jnp.maximum(total, 0.0)
        return total + pltpu.roll(total, 4, 0)

    def layer_one(store, first_q):
        for inner in range(STEPS):
            q = first_q + inner
            left = volume[pl.ds(q * 4, 4)].reshape(4 * COLUMN, 128)
            right = volume[pl.ds(q * 4 + 2, 4)].reshape(4 * COLUMN, 128)
            stacked = jnp.concatenate([left, right], axis=1)
            hidden = jnp.dot(w1[...], stacked, preferred_element_type=F32)
            high, low = split(jnp.maximum(hidden, 0.0))
            store[inner, 0] = high
            store[inner, 1] = low

    def layer_two(store, first_q, carry):
        for inner in range(STEPS):
            q = first_q + inner
            mixed = jnp.dot(w2[...], store[inner, 0], preferred_element_type=F32)
            found = mixed[:48] + mixed[48:]
            found = found + jnp.dot(w2[:48, :], store[inner, 1], preferred_element_type=F32)
            before = [found[8 * d : 8 * d + 8] for d in range(3)]
            behind = [found[24 + 8 * d : 32 + 8 * d] for d in range(3)]
            even = finish([before[d][:, :128] + carry[d] for d in range(3)])
            odd = finish([before[d][:, 128:] + behind[d][:, :128] for d in range(3)])
            carry = tuple(behind[d][:, 128:] for d in range(3))
            sublanes = lax.broadcasted_iota(jnp.int32, even.shape, 0)
            cons[pl.ds(pl.multiple_of(q * 8, 8), 8), :] = jnp.where(sublanes < 4, even, odd)
        return carry

    def layers(step, carry):
        q = step * 2 * STEPS
        layer_one(hidden_odd, q + STEPS)
        carry = layer_two(hidden_even, q, carry)
        layer_one(hidden_even, q + 2 * STEPS)
        return layer_two(hidden_odd, q + STEPS, carry)

    layer_one(hidden_even, 0)
    nothing = jnp.zeros((8, 128), F32)
    carry = lax.fori_loop(0, cells // (8 * STEPS), layers, (nothing,) * 3)
    cons[2 * cells : 2 * cells + 8, :] = finish(list(carry))

    rows_of = [cons[pl.ds(2 + k, cells, stride=2), :] for k in range(2)]
    best_row = jnp.max(jnp.transpose(jnp.maximum(*rows_of)), axis=0, keepdims=True)
    best_two[me] = best_row
    start_all(*two)
    scaled = [
        value * (value * (1.0 / (jnp.max(value, axis=0, keepdims=True) + EPSILON)))
        for value in rows_of
    ]

    gather_to(sibling).wait_send()
    lax.fori_loop(1, n // 2, gather_sent, 0)
    sent_all(*one)

    @pl.when(jnp.logical_not(last))
    def _():
        halo_up().wait_send()

    @pl.when(jnp.logical_not(first))
    def _():
        halo_down().wait_send()

    receive_all(*two)
    final_scale = 1.0 / (across(jnp.max(best_two[...], axis=0)) + EPSILON)
    for k in range(2):
        out_ref[pl.ds(k, cells, stride=2), :] = scaled[k] * (rows_of[k] * final_scale)
    sent_all(*two)


def shards(source_features, target_features, conv_first, conv_second):
    n = lax.axis_size("tgt")
    rows, channels = source_features.shape
    local_rows, width = target_features.shape[:2]
    cells = rows * n
    hidden = conv_first.shape[0]
    assert local_rows == 2 and width == 128 and cells == 128 and hidden == 16
    padded_rows = -(-rows // 8) * 8
    if padded_rows != rows:
        source_features = jnp.pad(source_features, ((0, padded_rows - rows), (0, 0)))
    selectors = (jnp.asarray(first_selector(), BF16), jnp.asarray(second_selector(), BF16))
    operands = (
        source_features,
        target_features.reshape(local_rows * width, channels),
        jnp.transpose(conv_first, (1, 2, 3, 4, 0)).reshape(27, 3, hidden),
        jnp.transpose(conv_second, (1, 2, 3, 4, 0)).reshape(27, 3, hidden),
        *selectors,
    )
    dma = pltpu.SemaphoreType.DMA
    result = pl.pallas_call(
        functools.partial(kernel, n, rows, cells),
        out_shape=jax.ShapeDtypeStruct((cells * local_rows, width), F32),
        in_specs=[pl.BlockSpec(memory_space=pl.ANY)] * len(operands),
        out_specs=pl.BlockSpec(memory_space=pltpu.VMEM),
        scratch_shapes=[
            *[pltpu.VMEM(operand.shape, operand.dtype) for operand in operands],
            pltpu.VMEM((2, 128, 128), F32),
            pltpu.VMEM((n, 2 * padded_rows, channels // 2), BF16),
            pltpu.VMEM((local_rows * width, channels), BF16),
            pltpu.VMEM((cells, local_rows * width), F32),
            pltpu.VMEM((2, cells, local_rows * width), F32),
            pltpu.VMEM((n, 1, 128), F32),
            pltpu.VMEM((n, 1, 128), F32),
            pltpu.VMEM((cells * SPAN, width), F32),
            pltpu.VMEM((cells, 128), F32),
            pltpu.VMEM((cells + 2 + 4 * STEPS, COLUMN, width), BF16),
            pltpu.VMEM((STEPS, 2, 256, 256), BF16),
            pltpu.VMEM((STEPS, 2, 256, 256), BF16),
            pltpu.VMEM((cells * 2 + 8, width), F32),
            pltpu.VMEM((256, 256), BF16),
            pltpu.VMEM((96, 256), BF16),
            dma((len(operands),)), dma((n,)), dma((n,)), dma((n,)), dma((2,)), dma((2,)),
            dma((n,)), dma((n,)), dma((n,)), dma((n,)),
        ],
        compiler_params=pltpu.CompilerParams(
            collective_id=0, has_side_effects=True, vmem_limit_bytes=VMEM_BYTES
        ),
        cost_estimate=pl.CostEstimate(
            flops=2 * 10**9, bytes_accessed=3 * 10**6, transcendentals=0
        ),
    )(*operands)
    return result.reshape(1, cells, local_rows, width)


def solution(mesh):
    placed = (P(("pairs", "tgt"), None), P(("pairs", "tgt"), None, None), P(), P())
    return jax.shard_map(
        shards, mesh=mesh, in_specs=placed, out_specs=P("pairs", None, "tgt", None), check_vma=False
    )
```

```python
import functools

import jax
import jax.numpy as jnp
import numpy as np
from jax import lax
from jax.experimental import pallas as pl
from jax.experimental.pallas import tpu as pltpu
from jax.sharding import PartitionSpec as P

EPSILON = 1e-05
MESH = pl.DeviceIdType.MESH
F32 = jnp.float32
BF16 = jnp.bfloat16
STEPS = 2
VMEM_BYTES = 63 * 1024 * 1024
COLUMN = 64
GROUP = 6
SPAN = 24


def place_of(part, d):
    if part < 2:
        return part * SPAN + d * GROUP
    return 3 * GROUP if d == 2 else 2 * SPAN + d * GROUP


def tap_number(branch, b, c, d):
    tap = 27 + 9 * b + 3 * c + d if branch == 0 else 27 * c + 9 * d + 3 + b
    return tap // 3 * 4 + tap % 3


def first_selector():
    table = np.zeros((2, 256, 256), np.float32)
    for branch in range(2):
        for b in range(3):
            for c in range(3):
                for d in range(3):
                    tap = tap_number(branch, b, c, d)
                    for part in range(3):
                        row = tap + (128 if part == 2 else 0)
                        column = b * COLUMN + place_of(part, d) + c
                        table[branch, row, column] = 1
    return table


def second_selector():
    table = np.zeros((2, 128, 1024), np.float32)
    for branch in range(2):
        for jj in range(2):
            for r in range(4):
                for group in range(2):
                    for d in range(3):
                        for jo in range(2):
                            for k in range(2):
                                b = jj - jo + 2 - 2 * group
                                c = r - k
                                if 0 <= b <= 2 and 0 <= c <= 2:
                                    tap = tap_number(branch, b, c, d)
                                    column = group * 24 + d * 8 + branch * 4 + jo * 2 + k
                                    table[branch, tap, (jj * 4 + r) * 128 + column] = 1
    return table


def unit(features):
    positive = jnp.maximum(features.astype(F32), 0.0)
    total = jnp.sum(positive * positive, axis=-1, keepdims=True)
    return positive * (1.0 / jnp.sqrt(total + 1e-06))


def split(value):
    high = value.astype(BF16)
    low = (value - high.astype(F32)).astype(BF16)
    return high, low


def shift_right(value):
    lanes = lax.broadcasted_iota(jnp.int32, value.shape, 1)
    return jnp.where(lanes >= 1, pltpu.roll(value, 1, 1), 0.0)


def shift_left(value):
    width = value.shape[1]
    lanes = lax.broadcasted_iota(jnp.int32, value.shape, 1)
    return jnp.where(lanes < width - 1, pltpu.roll(value, width - 1, 1), 0.0)


def across(row):
    wide = jnp.broadcast_to(row, (128, 128))
    return jnp.transpose(wide)


def kernel(
    n, rows, cells,
    src_hbm, tgt_hbm, first_hbm, second_hbm, e1_hbm, e2_hbm, out_ref,
    tgt_ref, first_ref, second_ref, e1_ref, e2_ref, taps,
    gathered, target_unit, corr, halo, best_one, best_two, window, scales, volume, hidden_even, hidden_odd, cons, w1, w2,
    local_sem, gather_send, gather_recv, pass_send, halo_send, halo_recv,
    one_send, one_recv, two_send, two_recv,
):
    pair = lax.axis_index("pairs")
    me = lax.axis_index("tgt")

    def device(index):
        return (pair, index)

    def other(step):
        return lax.rem(me + step, n)

    loads = [
        pltpu.make_async_copy(far, near, local_sem.at[number])
        for number, (far, near) in enumerate(
            [
                (src_hbm, gathered.at[me]), (tgt_hbm, tgt_ref), (first_hbm, first_ref),
                (second_hbm, second_ref), (e1_hbm, e1_ref), (e2_hbm, e2_ref),
            ]
        )
    ]
    for load in loads:
        load.start()
    barrier = pltpu.get_barrier_semaphore()

    def greet(step, carry):
        pl.semaphore_signal(barrier, inc=1, device_id=device(other(step)), device_id_type=MESH)
        return carry

    lax.fori_loop(1, n, greet, 0)

    def spread(buffer, send, recv, step):
        to = other(step)
        return pltpu.make_async_remote_copy(
            src_ref=buffer.at[me], dst_ref=buffer.at[me],
            send_sem=send.at[to], recv_sem=recv.at[me],
            device_id=device(to), device_id_type=MESH,
        )

    def arriving(buffer, send, recv, step):
        source = other(step)
        return pltpu.make_async_remote_copy(
            src_ref=buffer.at[source], dst_ref=buffer.at[source],
            send_sem=send.at[source], recv_sem=recv.at[source],
            device_id=device(source), device_id_type=MESH,
        )

    def start_all(*buffers):
        def body(step, carry):
            spread(*buffers, step).start()
            return carry

        lax.fori_loop(1, n, body, 0)

    def receive_all(*buffers):
        def body(step, carry):
            arriving(*buffers, step).wait_recv()
            return carry

        lax.fori_loop(1, n, body, 0)

    def sent_all(*buffers):
        def body(step, carry):
            spread(*buffers, step).wait_send()
            return carry

        lax.fori_loop(1, n, body, 0)

    one = (best_one, one_send, one_recv)
    two = (best_two, two_send, two_recv)

    pl.semaphore_wait(barrier, n - 1)

    sibling = me + 1 - 2 * lax.rem(me, 2)

    def gather_to(to):
        return pltpu.make_async_remote_copy(
            src_ref=src_hbm, dst_ref=gathered.at[me],
            send_sem=gather_send.at[to], recv_sem=gather_recv.at[me],
            device_id=device(to), device_id_type=MESH,
        )

    def pass_on(index):
        return pltpu.make_async_remote_copy(
            src_ref=gathered.at[index], dst_ref=gathered.at[index],
            send_sem=pass_send.at[index], recv_sem=gather_recv.at[index],
            device_id=device(sibling), device_id_type=MESH,
        )

    def gather_start(step, carry):
        gather_to(other(2 * step)).start()
        return carry

    def gather_pass(step, carry):
        index = lax.rem(me + n - 2 * step, n)
        pass_on(index).wait_recv()
        pass_on(index).start()
        return carry

    def gather_end(step, carry):
        pass_on(lax.rem(sibling + n - 2 * step, n)).wait_recv()
        return carry

    def gather_sent(step, carry):
        gather_to(other(2 * step)).wait_send()
        pass_on(lax.rem(me + n - 2 * step, n)).wait_send()
        return carry

    gather_to(sibling).start()
    lax.fori_loop(1, n // 2, gather_start, 0)

    loads[1].wait()
    target_unit[...] = unit(tgt_ref[...]).astype(BF16)
    lax.fori_loop(1, n // 2, gather_pass, 0)

    taps[...] = jnp.zeros(taps.shape, F32)
    for load in loads[2:]:
        load.wait()
    for number, weights in enumerate((first_ref, second_ref)):
        for tap in range(weights.shape[0]):
            taps[number, 4 * tap : 4 * tap + 3, 0:16] = weights[tap]
    first_high, first_low = split(jnp.transpose(taps[0])[:16])
    second_high, second_low = split(jnp.transpose(taps[1])[:16])
    first_parts = jnp.concatenate([first_high, first_low], axis=1)
    base = jnp.concatenate(
        [jnp.dot(first_parts, e1_ref[branch], preferred_element_type=F32) for branch in range(2)],
        axis=0,
    )
    for jj in range(2):
        for r in range(4):
            row = me * 2 - 1 + r
            inside = jnp.where(jnp.logical_and(row >= 0, row < n * 2), 1.0, 0.0).astype(F32)
            shift = jj * COLUMN + r
            moved = pltpu.roll(base, shift, 1) if shift else base
            start = (jj * 4 + r) * 32
            w1[start : start + 32, :] = (moved * inside).astype(BF16)
    second_parts = jnp.concatenate([second_high, second_low], axis=0)
    picked = [
        jnp.dot(second_parts, e2_ref[branch], preferred_element_type=F32) for branch in range(2)
    ]
    for part in range(2):
        blocks = []
        for number in range(8):
            for branch in range(2):
                blocks.append(
                    picked[branch][part * 16 : part * 16 + 16, number * 128 : number * 128 + 128]
                )
        turned = jnp.transpose(jnp.concatenate(blocks, axis=0))
        w2[part * 48 : part * 48 + 48, :] = turned[:48].astype(BF16)

    lax.fori_loop(0, n // 2, gather_end, 0)
    loads[0].wait()
    padded_rows, channels = gathered.shape[1:]
    everyone = gathered[...].astype(F32).reshape(n * padded_rows, channels)
    source = unit(everyone).astype(BF16)
    if rows != padded_rows:
        wanted = lax.broadcasted_iota(jnp.int32, (cells, n * padded_rows), 0)
        offered = lax.broadcasted_iota(jnp.int32, (cells, n * padded_rows), 1)
        place = (wanted // rows) * padded_rows + wanted % rows
        choice = jnp.where(place == offered, 1.0, 0.0).astype(BF16)
        source = jnp.dot(choice, source, preferred_element_type=F32).astype(BF16)
    products = lax.dot_general(
        source, target_unit[...], (((1,), (1,)), ((), ())), preferred_element_type=F32
    )
    corr[0] = products[:, :128]
    corr[1] = products[:, 128:]

    def halo_copy(side, row):
        to = lax.rem(me + 1, n) if side == 0 else lax.rem(me + n - 1, n)
        return pltpu.make_async_remote_copy(
            src_ref=corr.at[row], dst_ref=halo.at[side, row],
            send_sem=halo_send.at[side, row], recv_sem=halo_recv.at[side, row],
            device_id=device(to), device_id_type=MESH,
        )

    first, last = me == 0, me == n - 1

    @pl.when(jnp.logical_not(last))
    def _():
        halo_copy(0, 0).start()
        halo_copy(0, 1).start()

    @pl.when(jnp.logical_not(first))
    def _():
        halo_copy(1, 0).start()
        halo_copy(1, 1).start()

    local = jnp.maximum(corr[0], corr[1])
    best_row = jnp.max(jnp.transpose(local), axis=0, keepdims=True)
    best_one[me] = best_row
    start_all(*one)

    @pl.when(first)
    def _():
        halo[0] = jnp.zeros(halo.shape[1:], F32)

    @pl.when(last)
    def _():
        halo[1] = jnp.zeros(halo.shape[1:], F32)

    blank = jnp.zeros((COLUMN, 128), BF16)
    volume[0] = blank
    for extra in range(cells + 1, volume.shape[0]):
        volume[extra] = blank

    def place_row(slab, k):
        source_scale = 1.0 / (jnp.max(slab, axis=0, keepdims=True) + EPSILON)
        cubed = slab * (slab * source_scale) * slab
        after = shift_left(cubed)
        for group, value in enumerate((shift_right(cubed), cubed, after, after)):
            window[pl.ds(group * GROUP + k, cells, stride=SPAN), :] = value

    place_row(corr[0], 2)
    place_row(corr[1], 3)

    for row in range(2):

        @pl.when(jnp.logical_not(first))
        def _():
            halo_copy(0, row).wait_recv()

        @pl.when(jnp.logical_not(last))
        def _():
            halo_copy(1, row).wait_recv()

        for side in range(2):
            place_row(halo[side, row], side * 4 + row)

    receive_all(*one)
    scales[...] = 1.0 / (across(jnp.max(best_one[...], axis=0)) + EPSILON)

    def lay(step, carry):
        for inner in range(8):
            j = step * 8 + inner
            here = window[pl.ds(pl.multiple_of(j * SPAN, 8), SPAN), :] * scales[pl.ds(j, 1), :]
            high = here.astype(BF16).astype(F32)
            volume[j + 1] = jnp.concatenate([high, here - high, high[:16]], axis=0).astype(BF16)
        return carry

    lax.fori_loop(0, cells // 8, lay, 0)

    def finish(parts):
        total = shift_right(parts[0]) + parts[1] + shift_left(parts[2])
        total = jnp.maximum(total, 0.0)
        return total + pltpu.roll(total, 4, 0)

    def layer_one(store, first_q):
        for inner in range(STEPS):
            q = first_q + inner
            left = volume[pl.ds(q * 4, 4)].reshape(4 * COLUMN, 128)
            right = volume[pl.ds(q * 4 + 2, 4)].reshape(4 * COLUMN, 128)
            stacked = jnp.concatenate([left, right], axis=1)
            hidden = jnp.dot(w1[...], stacked, preferred_element_type=F32)
            high, low = split(jnp.maximum(hidden, 0.0))
            store[inner, 0] = high
            store[inner, 1] = low

    def layer_two(store, first_q, carry):
        for inner in range(STEPS):
            q = first_q + inner
            mixed = jnp.dot(w2[...], store[inner, 0], preferred_element_type=F32)
            found = mixed[:48] + mixed[48:]
            found = found + jnp.dot(w2[:48, :], store[inner, 1], preferred_element_type=F32)
            before = [found[8 * d : 8 * d + 8] for d in range(3)]
            behind = [found[24 + 8 * d : 32 + 8 * d] for d in range(3)]
            even = finish([before[d][:, :128] + carry[d] for d in range(3)])
            odd = finish([before[d][:, 128:] + behind[d][:, :128] for d in range(3)])
            carry = tuple(behind[d][:, 128:] for d in range(3))
            sublanes = lax.broadcasted_iota(jnp.int32, even.shape, 0)
            cons[pl.ds(pl.multiple_of(q * 8, 8), 8), :] = jnp.where(sublanes < 4, even, odd)
        return carry

    def layers(step, carry):
        q = step * 2 * STEPS
        layer_one(hidden_odd, q + STEPS)
        carry = layer_two(hidden_even, q, carry)
        layer_one(hidden_even, q + 2 * STEPS)
        return layer_two(hidden_odd, q + STEPS, carry)

    layer_one(hidden_even, 0)
    nothing = jnp.zeros((8, 128), F32)
    carry = lax.fori_loop(0, cells // (8 * STEPS), layers, (nothing,) * 3)
    cons[2 * cells : 2 * cells + 8, :] = finish(list(carry))

    rows_of = [cons[pl.ds(2 + k, cells, stride=2), :] for k in range(2)]
    best_row = jnp.max(jnp.transpose(jnp.maximum(*rows_of)), axis=0, keepdims=True)
    best_two[me] = best_row
    start_all(*two)
    scaled = [
        value * (value * (1.0 / (jnp.max(value, axis=0, keepdims=True) + EPSILON)))
        for value in rows_of
    ]

    gather_to(sibling).wait_send()
    lax.fori_loop(1, n // 2, gather_sent, 0)
    sent_all(*one)

    @pl.when(jnp.logical_not(last))
    def _():
        halo_copy(0, 0).wait_send()
        halo_copy(0, 1).wait_send()

    @pl.when(jnp.logical_not(first))
    def _():
        halo_copy(1, 0).wait_send()
        halo_copy(1, 1).wait_send()

    receive_all(*two)
    final_scale = 1.0 / (across(jnp.max(best_two[...], axis=0)) + EPSILON)
    for k in range(2):
        out_ref[pl.ds(k, cells, stride=2), :] = scaled[k] * (rows_of[k] * final_scale)
    sent_all(*two)


def shards(source_features, target_features, conv_first, conv_second):
    n = lax.axis_size("tgt")
    rows, channels = source_features.shape
    local_rows, width = target_features.shape[:2]
    cells = rows * n
    hidden = conv_first.shape[0]
    assert local_rows == 2 and width == 128 and cells == 128 and hidden == 16
    padded_rows = -(-rows // 8) * 8
    if padded_rows != rows:
        source_features = jnp.pad(source_features, ((0, padded_rows - rows), (0, 0)))
    selectors = (jnp.asarray(first_selector(), BF16), jnp.asarray(second_selector(), BF16))
    operands = (
        source_features,
        target_features.reshape(local_rows * width, channels),
        jnp.transpose(conv_first, (1, 2, 3, 4, 0)).reshape(27, 3, hidden),
        jnp.transpose(conv_second, (1, 2, 3, 4, 0)).reshape(27, 3, hidden),
        *selectors,
    )
    dma = pltpu.SemaphoreType.DMA
    result = pl.pallas_call(
        functools.partial(kernel, n, rows, cells),
        out_shape=pltpu.VMEM((cells * local_rows, width), F32),
        in_specs=[pl.BlockSpec(memory_space=pl.ANY)] * len(operands),
        out_specs=pl.BlockSpec(memory_space=pltpu.VMEM),
        scratch_shapes=[
            *[pltpu.VMEM(operand.shape, operand.dtype) for operand in operands[1:]],
            pltpu.VMEM((2, 128, 128), F32),
            pltpu.VMEM((n, padded_rows, channels), BF16),
            pltpu.VMEM((local_rows * width, channels), BF16),
            pltpu.VMEM((local_rows, cells, width), F32),
            pltpu.VMEM((2, local_rows, cells, width), F32),
            pltpu.VMEM((n, 1, 128), F32),
            pltpu.VMEM((n, 1, 128), F32),
            pltpu.VMEM((cells * SPAN, width), F32),
            pltpu.VMEM((cells, 128), F32),
            pltpu.VMEM((cells + 2 + 4 * STEPS, COLUMN, width), BF16),
            pltpu.VMEM((STEPS, 2, 256, 256), BF16),
            pltpu.VMEM((STEPS, 2, 256, 256), BF16),
            pltpu.VMEM((cells * 2 + 8, width), F32),
            pltpu.VMEM((256, 256), BF16),
            pltpu.VMEM((96, 256), BF16),
            dma((len(operands),)), dma((n,)), dma((n,)), dma((n,)), dma((2, 2)), dma((2, 2)),
            dma((n,)), dma((n,)), dma((n,)), dma((n,)),
        ],
        compiler_params=pltpu.CompilerParams(
            collective_id=0, has_side_effects=True, vmem_limit_bytes=VMEM_BYTES
        ),
        cost_estimate=pl.CostEstimate(
            flops=2 * 10**9, bytes_accessed=3 * 10**6, transcendentals=0
        ),
    )(*operands)
    return result.reshape(1, cells, local_rows, width)


def solution(mesh):
    placed = (P(("pairs", "tgt"), None), P(("pairs", "tgt"), None, None), P(), P())
    return jax.shard_map(
        shards, mesh=mesh, in_specs=placed, out_specs=P("pairs", None, "tgt", None), check_vma=False
    )
```

```python
import functools

import jax
import jax.numpy as jnp
import numpy as np
from jax import lax
from jax.experimental import pallas as pl
from jax.experimental.pallas import tpu as pltpu
from jax.sharding import PartitionSpec as P

EPSILON = 1e-05
MESH = pl.DeviceIdType.MESH
F32 = jnp.float32
BF16 = jnp.bfloat16
STEPS = 4
VMEM_BYTES = 63 * 1024 * 1024
COLUMN = 64
GROUP = 6
SPAN = 24


def place_of(part, d):
    if part < 2:
        return part * SPAN + d * GROUP
    return 3 * GROUP if d == 2 else 2 * SPAN + d * GROUP


def tap_number(branch, b, c, d):
    tap = 27 + 9 * b + 3 * c + d if branch == 0 else 27 * c + 9 * d + 3 + b
    return tap // 3 * 4 + tap % 3


def first_selector():
    table = np.zeros((2, 256, 256), np.float32)
    for branch in range(2):
        for b in range(3):
            for c in range(3):
                for d in range(3):
                    tap = tap_number(branch, b, c, d)
                    for part in range(3):
                        row = tap + (128 if part == 2 else 0)
                        column = b * COLUMN + place_of(part, d) + c
                        table[branch, row, column] = 1
    return table


def second_selector():
    table = np.zeros((2, 128, 1024), np.float32)
    for branch in range(2):
        for jj in range(2):
            for r in range(4):
                for group in range(2):
                    for d in range(3):
                        for jo in range(2):
                            for k in range(2):
                                b = jj - jo + 2 - 2 * group
                                c = r - k
                                if 0 <= b <= 2 and 0 <= c <= 2:
                                    tap = tap_number(branch, b, c, d)
                                    column = group * 24 + d * 8 + branch * 4 + jo * 2 + k
                                    table[branch, tap, (jj * 4 + r) * 128 + column] = 1
    return table


def unit(features):
    positive = jnp.maximum(features.astype(F32), 0.0)
    total = jnp.sum(positive * positive, axis=-1, keepdims=True)
    return positive * (1.0 / jnp.sqrt(total + 1e-06))


def split(value):
    high = value.astype(BF16)
    low = (value - high.astype(F32)).astype(BF16)
    return high, low


def shift_right(value):
    lanes = lax.broadcasted_iota(jnp.int32, value.shape, 1)
    return jnp.where(lanes >= 1, pltpu.roll(value, 1, 1), 0.0)


def shift_left(value):
    width = value.shape[1]
    lanes = lax.broadcasted_iota(jnp.int32, value.shape, 1)
    return jnp.where(lanes < width - 1, pltpu.roll(value, width - 1, 1), 0.0)


def across(row):
    wide = jnp.broadcast_to(row, (128, 128))
    return jnp.transpose(wide)


def kernel(
    n, rows, cells,
    src_hbm, tgt_hbm, first_hbm, second_hbm, e1_hbm, e2_hbm, out_ref,
    tgt_ref, first_ref, second_ref, e1_ref, e2_ref, taps,
    gathered, target_unit, corr, halo, best_one, best_two, window, scales, volume, hidden_even, hidden_odd, cons, w1, w2,
    local_sem, gather_send, gather_recv, pass_send, halo_send, halo_recv,
    one_send, one_recv, two_send, two_recv,
):
    pair = lax.axis_index("pairs")
    me = lax.axis_index("tgt")

    def device(index):
        return (pair, index)

    def other(step):
        return lax.rem(me + step, n)

    loads = [
        pltpu.make_async_copy(far, near, local_sem.at[number])
        for number, (far, near) in enumerate(
            [
                (src_hbm, gathered.at[me]), (tgt_hbm, tgt_ref), (first_hbm, first_ref),
                (second_hbm, second_ref), (e1_hbm, e1_ref), (e2_hbm, e2_ref),
            ]
        )
    ]
    for load in loads:
        load.start()
    barrier = pltpu.get_barrier_semaphore()

    def greet(step, carry):
        pl.semaphore_signal(barrier, inc=1, device_id=device(other(step)), device_id_type=MESH)
        return carry

    lax.fori_loop(1, n, greet, 0)

    def spread(buffer, send, recv, step):
        to = other(step)
        return pltpu.make_async_remote_copy(
            src_ref=buffer.at[me], dst_ref=buffer.at[me],
            send_sem=send.at[to], recv_sem=recv.at[me],
            device_id=device(to), device_id_type=MESH,
        )

    def arriving(buffer, send, recv, step):
        source = other(step)
        return pltpu.make_async_remote_copy(
            src_ref=buffer.at[source], dst_ref=buffer.at[source],
            send_sem=send.at[source], recv_sem=recv.at[source],
            device_id=device(source), device_id_type=MESH,
        )

    def start_all(*buffers):
        def body(step, carry):
            spread(*buffers, step).start()
            return carry

        lax.fori_loop(1, n, body, 0)

    def receive_all(*buffers):
        def body(step, carry):
            arriving(*buffers, step).wait_recv()
            return carry

        lax.fori_loop(1, n, body, 0)

    def sent_all(*buffers):
        def body(step, carry):
            spread(*buffers, step).wait_send()
            return carry

        lax.fori_loop(1, n, body, 0)

    one = (best_one, one_send, one_recv)
    two = (best_two, two_send, two_recv)

    pl.semaphore_wait(barrier, n - 1)

    sibling = me + 1 - 2 * lax.rem(me, 2)

    def gather_to(to):
        return pltpu.make_async_remote_copy(
            src_ref=src_hbm, dst_ref=gathered.at[me],
            send_sem=gather_send.at[to], recv_sem=gather_recv.at[me],
            device_id=device(to), device_id_type=MESH,
        )

    def pass_on(index):
        return pltpu.make_async_remote_copy(
            src_ref=gathered.at[index], dst_ref=gathered.at[index],
            send_sem=pass_send.at[index], recv_sem=gather_recv.at[index],
            device_id=device(sibling), device_id_type=MESH,
        )

    def gather_start(step, carry):
        gather_to(other(2 * step)).start()
        return carry

    def gather_pass(step, carry):
        index = lax.rem(me + n - 2 * step, n)
        pass_on(index).wait_recv()
        pass_on(index).start()
        return carry

    def gather_end(step, carry):
        pass_on(lax.rem(sibling + n - 2 * step, n)).wait_recv()
        return carry

    def gather_sent(step, carry):
        gather_to(other(2 * step)).wait_send()
        pass_on(lax.rem(me + n - 2 * step, n)).wait_send()
        return carry

    gather_to(sibling).start()
    lax.fori_loop(1, n // 2, gather_start, 0)

    loads[1].wait()
    target_unit[...] = unit(tgt_ref[...]).astype(BF16)
    lax.fori_loop(1, n // 2, gather_pass, 0)

    taps[...] = jnp.zeros(taps.shape, F32)
    for load in loads[2:]:
        load.wait()
    for number, weights in enumerate((first_ref, second_ref)):
        for tap in range(weights.shape[0]):
            taps[number, 4 * tap : 4 * tap + 3, 0:16] = weights[tap]
    first_high, first_low = split(jnp.transpose(taps[0])[:16])
    second_high, second_low = split(jnp.transpose(taps[1])[:16])
    first_parts = jnp.concatenate([first_high, first_low], axis=1)
    base = jnp.concatenate(
        [jnp.dot(first_parts, e1_ref[branch], preferred_element_type=F32) for branch in range(2)],
        axis=0,
    )
    for jj in range(2):
        for r in range(4):
            row = me * 2 - 1 + r
            inside = jnp.where(jnp.logical_and(row >= 0, row < n * 2), 1.0, 0.0).astype(F32)
            shift = jj * COLUMN + r
            moved = pltpu.roll(base, shift, 1) if shift else base
            start = (jj * 4 + r) * 32
            w1[start : start + 32, :] = (moved * inside).astype(BF16)
    second_parts = jnp.concatenate([second_high, second_low], axis=0)
    picked = [
        jnp.dot(second_parts, e2_ref[branch], preferred_element_type=F32) for branch in range(2)
    ]
    for part in range(2):
        blocks = []
        for number in range(8):
            for branch in range(2):
                blocks.append(
                    picked[branch][part * 16 : part * 16 + 16, number * 128 : number * 128 + 128]
                )
        turned = jnp.transpose(jnp.concatenate(blocks, axis=0))
        w2[part * 48 : part * 48 + 48, :] = turned[:48].astype(BF16)

    lax.fori_loop(0, n // 2, gather_end, 0)
    loads[0].wait()
    padded_rows, channels = gathered.shape[1:]
    everyone = gathered[...].astype(F32).reshape(n * padded_rows, channels)
    source = unit(everyone).astype(BF16)
    if rows != padded_rows:
        wanted = lax.broadcasted_iota(jnp.int32, (cells, n * padded_rows), 0)
        offered = lax.broadcasted_iota(jnp.int32, (cells, n * padded_rows), 1)
        place = (wanted // rows) * padded_rows + wanted % rows
        choice = jnp.where(place == offered, 1.0, 0.0).astype(BF16)
        source = jnp.dot(choice, source, preferred_element_type=F32).astype(BF16)
    products = lax.dot_general(
        source, target_unit[...], (((1,), (1,)), ((), ())), preferred_element_type=F32
    )
    corr[0] = products[:, :128]
    corr[1] = products[:, 128:]

    def halo_copy(side, row):
        to = lax.rem(me + 1, n) if side == 0 else lax.rem(me + n - 1, n)
        return pltpu.make_async_remote_copy(
            src_ref=corr.at[row], dst_ref=halo.at[side, row],
            send_sem=halo_send.at[side, row], recv_sem=halo_recv.at[side, row],
            device_id=device(to), device_id_type=MESH,
        )

    first, last = me == 0, me == n - 1

    @pl.when(jnp.logical_not(last))
    def _():
        halo_copy(0, 0).start()
        halo_copy(0, 1).start()

    @pl.when(jnp.logical_not(first))
    def _():
        halo_copy(1, 0).start()
        halo_copy(1, 1).start()

    local = jnp.maximum(corr[0], corr[1])
    best_row = jnp.max(jnp.transpose(local), axis=0, keepdims=True)
    best_one[me] = best_row
    start_all(*one)

    @pl.when(first)
    def _():
        halo[0] = jnp.zeros(halo.shape[1:], F32)

    @pl.when(last)
    def _():
        halo[1] = jnp.zeros(halo.shape[1:], F32)

    volume[0] = jnp.zeros((COLUMN, 128), BF16)
    window[cells * SPAN :, :] = jnp.zeros((SPAN, 128), F32)
    scales[cells:, :] = jnp.zeros((8, 128), F32)

    def place_row(slab, k):
        source_scale = 1.0 / (jnp.max(slab, axis=0, keepdims=True) + EPSILON)
        cubed = slab * (slab * source_scale) * slab
        after = shift_left(cubed)
        for group, value in enumerate((shift_right(cubed), cubed, after, after)):
            window[pl.ds(group * GROUP + k, cells, stride=SPAN), :] = value

    place_row(corr[0], 2)
    place_row(corr[1], 3)

    for row in range(2):

        @pl.when(jnp.logical_not(first))
        def _():
            halo_copy(0, row).wait_recv()

        @pl.when(jnp.logical_not(last))
        def _():
            halo_copy(1, row).wait_recv()

        for side in range(2):
            place_row(halo[side, row], side * 4 + row)

    receive_all(*one)
    scales[0:cells, :] = 1.0 / (across(jnp.max(best_one[...], axis=0)) + EPSILON)

    def lay(j):
        here = window[pl.ds(pl.multiple_of(j * SPAN, 8), SPAN), :] * scales[pl.ds(j, 1), :]
        high = here.astype(BF16).astype(F32)
        volume[j + 1] = jnp.concatenate([high, here - high, high[:16]], axis=0).astype(BF16)

    def lay_block(first_q):
        for inner in range(4 * STEPS):
            lay(first_q * 4 + 1 + inner)

    def finish(parts):
        total = shift_right(parts[0]) + parts[1] + shift_left(parts[2])
        total = jnp.maximum(total, 0.0)
        return total + pltpu.roll(total, 4, 0)

    def layer_one(store, first_q):
        for inner in range(STEPS):
            q = first_q + inner
            left = volume[pl.ds(q * 4, 4)].reshape(4 * COLUMN, 128)
            right = volume[pl.ds(q * 4 + 2, 4)].reshape(4 * COLUMN, 128)
            stacked = jnp.concatenate([left, right], axis=1)
            hidden = jnp.dot(w1[...], stacked, preferred_element_type=F32)
            high, low = split(jnp.maximum(hidden, 0.0))
            store[inner, 0] = high
            store[inner, 1] = low

    def layer_two(store, first_q, carry):
        for inner in range(STEPS):
            q = first_q + inner
            mixed = jnp.dot(w2[...], store[inner, 0], preferred_element_type=F32)
            found = mixed[:48] + mixed[48:]
            found = found + jnp.dot(w2[:48, :], store[inner, 1], preferred_element_type=F32)
            before = [found[8 * d : 8 * d + 8] for d in range(3)]
            behind = [found[24 + 8 * d : 32 + 8 * d] for d in range(3)]
            even = finish([before[d][:, :128] + carry[d] for d in range(3)])
            odd = finish([before[d][:, 128:] + behind[d][:, :128] for d in range(3)])
            carry = tuple(behind[d][:, 128:] for d in range(3))
            sublanes = lax.broadcasted_iota(jnp.int32, even.shape, 0)
            cons[pl.ds(pl.multiple_of(q * 8, 8), 8), :] = jnp.where(sublanes < 4, even, odd)
        return carry

    def layers(step, carry):
        q = step * 2 * STEPS
        layer_one(hidden_odd, q + STEPS)
        carry = layer_two(hidden_even, q, carry)
        lay_block(q + 2 * STEPS)
        layer_one(hidden_even, q + 2 * STEPS)
        carry = layer_two(hidden_odd, q + STEPS, carry)
        lay_block(q + 3 * STEPS)
        return carry

    lay(0)
    lay_block(0)
    lay_block(STEPS)
    layer_one(hidden_even, 0)
    nothing = jnp.zeros((8, 128), F32)
    carry = lax.fori_loop(0, cells // (8 * STEPS) - 1, layers, (nothing,) * 3)
    last_q = cells // 4 - STEPS
    layer_one(hidden_odd, last_q)
    carry = layer_two(hidden_even, last_q - STEPS, carry)
    carry = layer_two(hidden_odd, last_q, carry)
    cons[2 * cells : 2 * cells + 8, :] = finish(list(carry))

    rows_of = [cons[pl.ds(2 + k, cells, stride=2), :] for k in range(2)]
    best_row = jnp.max(jnp.transpose(jnp.maximum(*rows_of)), axis=0, keepdims=True)
    best_two[me] = best_row
    start_all(*two)
    scaled = [
        value * (value * (1.0 / (jnp.max(value, axis=0, keepdims=True) + EPSILON)))
        for value in rows_of
    ]

    gather_to(sibling).wait_send()
    lax.fori_loop(1, n // 2, gather_sent, 0)
    sent_all(*one)

    @pl.when(jnp.logical_not(last))
    def _():
        halo_copy(0, 0).wait_send()
        halo_copy(0, 1).wait_send()

    @pl.when(jnp.logical_not(first))
    def _():
        halo_copy(1, 0).wait_send()
        halo_copy(1, 1).wait_send()

    receive_all(*two)
    final_scale = 1.0 / (across(jnp.max(best_two[...], axis=0)) + EPSILON)
    for k in range(2):
        out_ref[pl.ds(k, cells, stride=2), :] = scaled[k] * (rows_of[k] * final_scale)
    sent_all(*two)


def shards(source_features, target_features, conv_first, conv_second):
    n = lax.axis_size("tgt")
    rows, channels = source_features.shape
    local_rows, width = target_features.shape[:2]
    cells = rows * n
    hidden = conv_first.shape[0]
    assert local_rows == 2 and width == 128 and cells == 128 and hidden == 16
    padded_rows = -(-rows // 8) * 8
    if padded_rows != rows:
        source_features = jnp.pad(source_features, ((0, padded_rows - rows), (0, 0)))
    selectors = (jnp.asarray(first_selector(), BF16), jnp.asarray(second_selector(), BF16))
    operands = (
        source_features,
        target_features.reshape(local_rows * width, channels),
        jnp.transpose(conv_first, (1, 2, 3, 4, 0)).reshape(27, 3, hidden),
        jnp.transpose(conv_second, (1, 2, 3, 4, 0)).reshape(27, 3, hidden),
        *selectors,
    )
    dma = pltpu.SemaphoreType.DMA
    result = pl.pallas_call(
        functools.partial(kernel, n, rows, cells),
        out_shape=pltpu.VMEM((cells * local_rows, width), F32),
        in_specs=[pl.BlockSpec(memory_space=pl.ANY)] * len(operands),
        out_specs=pl.BlockSpec(memory_space=pltpu.VMEM),
        scratch_shapes=[
            *[pltpu.VMEM(operand.shape, operand.dtype) for operand in operands[1:]],
            pltpu.VMEM((2, 128, 128), F32),
            pltpu.VMEM((n, padded_rows, channels), BF16),
            pltpu.VMEM((local_rows * width, channels), BF16),
            pltpu.VMEM((local_rows, cells, width), F32),
            pltpu.VMEM((2, local_rows, cells, width), F32),
            pltpu.VMEM((n, 1, 128), F32),
            pltpu.VMEM((n, 1, 128), F32),
            pltpu.VMEM(((cells + 1) * SPAN, width), F32),
            pltpu.VMEM((cells + 8, 128), F32),
            pltpu.VMEM((cells + 2, COLUMN, width), BF16),
            pltpu.VMEM((STEPS, 2, 256, 256), BF16),
            pltpu.VMEM((STEPS, 2, 256, 256), BF16),
            pltpu.VMEM((cells * 2 + 8, width), F32),
            pltpu.VMEM((256, 256), BF16),
            pltpu.VMEM((96, 256), BF16),
            dma((len(operands),)), dma((n,)), dma((n,)), dma((n,)), dma((2, 2)), dma((2, 2)),
            dma((n,)), dma((n,)), dma((n,)), dma((n,)),
        ],
        compiler_params=pltpu.CompilerParams(
            collective_id=0, has_side_effects=True, vmem_limit_bytes=VMEM_BYTES
        ),
        cost_estimate=pl.CostEstimate(
            flops=2 * 10**9, bytes_accessed=3 * 10**6, transcendentals=0
        ),
    )(*operands)
    return result.reshape(1, cells, local_rows, width)


def solution(mesh):
    placed = (P(("pairs", "tgt"), None), P(("pairs", "tgt"), None, None), P(), P())
    return jax.shard_map(
        shards, mesh=mesh, in_specs=placed, out_specs=P("pairs", None, "tgt", None), check_vma=False
    )
```

```python
import functools

import jax
import jax.numpy as jnp
import numpy as np
from jax import lax
from jax.experimental import pallas as pl
from jax.experimental.pallas import tpu as pltpu
from jax.sharding import PartitionSpec as P

EPSILON = 1e-05
MESH = pl.DeviceIdType.MESH
F32 = jnp.float32
BF16 = jnp.bfloat16
STEPS = 4
VMEM_BYTES = 63 * 1024 * 1024
COLUMN = 64
GROUP = 6
SPAN = 24


def place_of(part, d):
    if part < 2:
        return part * SPAN + d * GROUP
    return 3 * GROUP if d == 2 else 2 * SPAN + d * GROUP


def tap_number(branch, b, c, d):
    tap = 27 + 9 * b + 3 * c + d if branch == 0 else 27 * c + 9 * d + 3 + b
    return tap // 3 * 4 + tap % 3


def first_selector():
    table = np.zeros((2, 256, 256), np.float32)
    for branch in range(2):
        for b in range(3):
            for c in range(3):
                for d in range(3):
                    tap = tap_number(branch, b, c, d)
                    for part in range(3):
                        row = tap + (128 if part == 2 else 0)
                        column = b * COLUMN + place_of(part, d) + c
                        table[branch, row, column] = 1
    return table


def second_selector():
    table = np.zeros((2, 128, 1024), np.float32)
    for branch in range(2):
        for jj in range(2):
            for r in range(4):
                for group in range(2):
                    for d in range(3):
                        for jo in range(2):
                            for k in range(2):
                                b = jj - jo + 2 - 2 * group
                                c = r - k
                                if 0 <= b <= 2 and 0 <= c <= 2:
                                    tap = tap_number(branch, b, c, d)
                                    column = group * 24 + d * 8 + branch * 4 + jo * 2 + k
                                    table[branch, tap, (jj * 4 + r) * 128 + column] = 1
    return table


def unit(features):
    positive = jnp.maximum(features.astype(F32), 0.0)
    total = jnp.sum(positive * positive, axis=-1, keepdims=True)
    return positive * (1.0 / jnp.sqrt(total + 1e-06))


def split(value):
    high = value.astype(BF16)
    low = (value - high.astype(F32)).astype(BF16)
    return high, low


def shift_right(value):
    lanes = lax.broadcasted_iota(jnp.int32, value.shape, 1)
    return jnp.where(lanes >= 1, pltpu.roll(value, 1, 1), 0.0)


def shift_left(value):
    width = value.shape[1]
    lanes = lax.broadcasted_iota(jnp.int32, value.shape, 1)
    return jnp.where(lanes < width - 1, pltpu.roll(value, width - 1, 1), 0.0)


def across(row):
    wide = jnp.broadcast_to(row, (128, 128))
    return jnp.transpose(wide)


def kernel(
    n, rows, cells,
    src_hbm, tgt_hbm, first_hbm, second_hbm, e1_hbm, e2_hbm, out_ref,
    tgt_ref, first_ref, second_ref, e1_ref, e2_ref, taps,
    gathered, target_unit, corr, halo, best_one, best_two, window, scales, volume, hidden_even, hidden_odd, cons, w1, w2,
    local_sem, gather_send, gather_recv, pass_send, halo_send, halo_recv,
    one_send, one_recv, two_send, two_recv,
):
    pair = lax.axis_index("pairs")
    me = lax.axis_index("tgt")

    def device(index):
        return (pair, index)

    def other(step):
        return lax.rem(me + step, n)

    loads = [
        pltpu.make_async_copy(far, near, local_sem.at[number])
        for number, (far, near) in enumerate(
            [
                (src_hbm, gathered.at[me]), (tgt_hbm, tgt_ref), (first_hbm, first_ref),
                (second_hbm, second_ref), (e1_hbm, e1_ref), (e2_hbm, e2_ref),
            ]
        )
    ]
    for load in loads:
        load.start()
    barrier = pltpu.get_barrier_semaphore()

    def greet(step, carry):
        pl.semaphore_signal(barrier, inc=1, device_id=device(other(step)), device_id_type=MESH)
        return carry

    lax.fori_loop(1, n, greet, 0)

    def spread(buffer, send, recv, step):
        to = other(step)
        return pltpu.make_async_remote_copy(
            src_ref=buffer.at[me], dst_ref=buffer.at[me],
            send_sem=send.at[to], recv_sem=recv.at[me],
            device_id=device(to), device_id_type=MESH,
        )

    def arriving(buffer, send, recv, step):
        source = other(step)
        return pltpu.make_async_remote_copy(
            src_ref=buffer.at[source], dst_ref=buffer.at[source],
            send_sem=send.at[source], recv_sem=recv.at[source],
            device_id=device(source), device_id_type=MESH,
        )

    def start_all(*buffers):
        def body(step, carry):
            spread(*buffers, step).start()
            return carry

        lax.fori_loop(1, n, body, 0)

    def receive_all(*buffers):
        def body(step, carry):
            arriving(*buffers, step).wait_recv()
            return carry

        lax.fori_loop(1, n, body, 0)

    def sent_all(*buffers):
        def body(step, carry):
            spread(*buffers, step).wait_send()
            return carry

        lax.fori_loop(1, n, body, 0)

    one = (best_one, one_send, one_recv)
    two = (best_two, two_send, two_recv)

    pl.semaphore_wait(barrier, n - 1)

    sibling = me + 1 - 2 * lax.rem(me, 2)

    def gather_to(to):
        return pltpu.make_async_remote_copy(
            src_ref=src_hbm, dst_ref=gathered.at[me],
            send_sem=gather_send.at[to], recv_sem=gather_recv.at[me],
            device_id=device(to), device_id_type=MESH,
        )

    def pass_on(index):
        return pltpu.make_async_remote_copy(
            src_ref=gathered.at[index], dst_ref=gathered.at[index],
            send_sem=pass_send.at[index], recv_sem=gather_recv.at[index],
            device_id=device(sibling), device_id_type=MESH,
        )

    def gather_start(step, carry):
        gather_to(other(2 * step)).start()
        return carry

    def gather_pass(step, carry):
        index = lax.rem(me + n - 2 * step, n)
        pass_on(index).wait_recv()
        pass_on(index).start()
        return carry

    def gather_end(step, carry):
        pass_on(lax.rem(sibling + n - 2 * step, n)).wait_recv()
        return carry

    def gather_sent(step, carry):
        gather_to(other(2 * step)).wait_send()
        pass_on(lax.rem(me + n - 2 * step, n)).wait_send()
        return carry

    gather_to(sibling).start()
    lax.fori_loop(1, n // 2, gather_start, 0)

    loads[1].wait()
    target_unit[...] = unit(tgt_ref[...]).astype(BF16)
    lax.fori_loop(1, n // 2, gather_pass, 0)

    taps[...] = jnp.zeros(taps.shape, F32)
    for load in loads[2:]:
        load.wait()
    for number, weights in enumerate((first_ref, second_ref)):
        for tap in range(weights.shape[0]):
            taps[number, 4 * tap : 4 * tap + 3, 0:16] = weights[tap]
    first_high, first_low = split(jnp.transpose(taps[0])[:16])
    second_high, second_low = split(jnp.transpose(taps[1])[:16])
    first_parts = jnp.concatenate([first_high, first_low], axis=1)
    base = jnp.concatenate(
        [jnp.dot(first_parts, e1_ref[branch], preferred_element_type=F32) for branch in range(2)],
        axis=0,
    )
    for jj in range(2):
        for r in range(4):
            row = me * 2 - 1 + r
            inside = jnp.where(jnp.logical_and(row >= 0, row < n * 2), 1.0, 0.0).astype(F32)
            shift = jj * COLUMN + r
            moved = pltpu.roll(base, shift, 1) if shift else base
            start = (jj * 4 + r) * 32
            w1[start : start + 32, :] = (moved * inside).astype(BF16)
    second_parts = jnp.concatenate([second_high, second_low], axis=0)
    picked = [
        jnp.dot(second_parts, e2_ref[branch], preferred_element_type=F32) for branch in range(2)
    ]
    for part in range(2):
        blocks = []
        for number in range(8):
            for branch in range(2):
                blocks.append(
                    picked[branch][part * 16 : part * 16 + 16, number * 128 : number * 128 + 128]
                )
        turned = jnp.transpose(jnp.concatenate(blocks, axis=0))
        w2[part * 48 : part * 48 + 48, :] = turned[:48].astype(BF16)

    lax.fori_loop(0, n // 2, gather_end, 0)
    loads[0].wait()
    padded_rows, channels = gathered.shape[1:]
    everyone = gathered[...].astype(F32).reshape(n * padded_rows, channels)
    source = unit(everyone).astype(BF16)
    if rows != padded_rows:
        wanted = lax.broadcasted_iota(jnp.int32, (cells, n * padded_rows), 0)
        offered = lax.broadcasted_iota(jnp.int32, (cells, n * padded_rows), 1)
        place = (wanted // rows) * padded_rows + wanted % rows
        choice = jnp.where(place == offered, 1.0, 0.0).astype(BF16)
        source = jnp.dot(choice, source, preferred_element_type=F32).astype(BF16)
    products = lax.dot_general(
        source, target_unit[...], (((1,), (1,)), ((), ())), preferred_element_type=F32
    )
    corr[0] = products[:, :128]
    corr[1] = products[:, 128:]

    def halo_copy(side, row):
        to = lax.rem(me + 1, n) if side == 0 else lax.rem(me + n - 1, n)
        return pltpu.make_async_remote_copy(
            src_ref=corr.at[row], dst_ref=halo.at[side, row],
            send_sem=halo_send.at[side, row], recv_sem=halo_recv.at[side, row],
            device_id=device(to), device_id_type=MESH,
        )

    first, last = me == 0, me == n - 1

    local = jnp.maximum(corr[0], corr[1])
    best_row = jnp.max(jnp.transpose(local), axis=0, keepdims=True)
    best_one[me] = best_row
    start_all(*one)

    @pl.when(jnp.logical_not(last))
    def _():
        halo_copy(0, 0).start()
        halo_copy(0, 1).start()

    @pl.when(jnp.logical_not(first))
    def _():
        halo_copy(1, 0).start()
        halo_copy(1, 1).start()


    @pl.when(first)
    def _():
        halo[0] = jnp.zeros(halo.shape[1:], F32)

    @pl.when(last)
    def _():
        halo[1] = jnp.zeros(halo.shape[1:], F32)

    volume[0] = jnp.zeros((COLUMN, 128), BF16)
    window[cells * SPAN :, :] = jnp.zeros((SPAN, 128), F32)
    scales[cells:, :] = jnp.zeros((8, 128), F32)

    def place_row(slab, k):
        source_scale = 1.0 / (jnp.max(slab, axis=0, keepdims=True) + EPSILON)
        cubed = slab * (slab * source_scale) * slab
        after = shift_left(cubed)
        for group, value in enumerate((shift_right(cubed), cubed, after, after)):
            window[pl.ds(group * GROUP + k, cells, stride=SPAN), :] = value

    place_row(corr[0], 2)
    place_row(corr[1], 3)

    for row in range(2):

        @pl.when(jnp.logical_not(first))
        def _():
            halo_copy(0, row).wait_recv()

        @pl.when(jnp.logical_not(last))
        def _():
            halo_copy(1, row).wait_recv()

        for side in range(2):
            place_row(halo[side, row], side * 4 + row)

    receive_all(*one)
    scales[0:cells, :] = 1.0 / (across(jnp.max(best_one[...], axis=0)) + EPSILON)

    def lay(j):
        here = window[pl.ds(pl.multiple_of(j * SPAN, 8), SPAN), :] * scales[pl.ds(j, 1), :]
        high = here.astype(BF16).astype(F32)
        volume[j + 1] = jnp.concatenate([high, here - high, high[:16]], axis=0).astype(BF16)

    def lay_block(first_q):
        for inner in range(4 * STEPS):
            lay(first_q * 4 + 1 + inner)

    def finish(parts):
        total = shift_right(parts[0]) + parts[1] + shift_left(parts[2])
        total = jnp.maximum(total, 0.0)
        return total + pltpu.roll(total, 4, 0)

    def layer_one(store, first_q):
        for inner in range(STEPS):
            q = first_q + inner
            left = volume[pl.ds(q * 4, 4)].reshape(4 * COLUMN, 128)
            right = volume[pl.ds(q * 4 + 2, 4)].reshape(4 * COLUMN, 128)
            stacked = jnp.concatenate([left, right], axis=1)
            hidden = jnp.dot(w1[...], stacked, preferred_element_type=F32)
            high, low = split(jnp.maximum(hidden, 0.0))
            store[inner, 0] = high
            store[inner, 1] = low

    def layer_two(store, first_q, carry):
        for inner in range(STEPS):
            q = first_q + inner
            mixed = jnp.dot(w2[...], store[inner, 0], preferred_element_type=F32)
            found = mixed[:48] + mixed[48:]
            found = found + jnp.dot(w2[:48, :], store[inner, 1], preferred_element_type=F32)
            before = [found[8 * d : 8 * d + 8] for d in range(3)]
            behind = [found[24 + 8 * d : 32 + 8 * d] for d in range(3)]
            even = finish([before[d][:, :128] + carry[d] for d in range(3)])
            odd = finish([before[d][:, 128:] + behind[d][:, :128] for d in range(3)])
            carry = tuple(behind[d][:, 128:] for d in range(3))
            sublanes = lax.broadcasted_iota(jnp.int32, even.shape, 0)
            cons[pl.ds(pl.multiple_of(q * 8, 8), 8), :] = jnp.where(sublanes < 4, even, odd)
        return carry

    def layers(step, carry):
        q = step * 2 * STEPS
        layer_one(hidden_odd, q + STEPS)
        carry = layer_two(hidden_even, q, carry)
        lay_block(q + 2 * STEPS)
        layer_one(hidden_even, q + 2 * STEPS)
        carry = layer_two(hidden_odd, q + STEPS, carry)
        lay_block(q + 3 * STEPS)
        return carry

    lay(0)
    lay_block(0)
    lay_block(STEPS)
    layer_one(hidden_even, 0)
    nothing = jnp.zeros((8, 128), F32)
    carry = lax.fori_loop(0, cells // (8 * STEPS) - 1, layers, (nothing,) * 3)
    last_q = cells // 4 - STEPS
    layer_one(hidden_odd, last_q)
    carry = layer_two(hidden_even, last_q - STEPS, carry)
    carry = layer_two(hidden_odd, last_q, carry)
    cons[2 * cells : 2 * cells + 8, :] = finish(list(carry))

    rows_of = [cons[pl.ds(2 + k, cells, stride=2), :] for k in range(2)]
    best_row = jnp.max(jnp.transpose(jnp.maximum(*rows_of)), axis=0, keepdims=True)
    best_two[me] = best_row
    start_all(*two)
    scaled = [
        value * (value * (1.0 / (jnp.max(value, axis=0, keepdims=True) + EPSILON)))
        for value in rows_of
    ]

    gather_to(sibling).wait_send()
    lax.fori_loop(1, n // 2, gather_sent, 0)
    sent_all(*one)

    @pl.when(jnp.logical_not(last))
    def _():
        halo_copy(0, 0).wait_send()
        halo_copy(0, 1).wait_send()

    @pl.when(jnp.logical_not(first))
    def _():
        halo_copy(1, 0).wait_send()
        halo_copy(1, 1).wait_send()

    receive_all(*two)
    final_scale = 1.0 / (across(jnp.max(best_two[...], axis=0)) + EPSILON)
    for k in range(2):
        out_ref[pl.ds(k, cells, stride=2), :] = scaled[k] * (rows_of[k] * final_scale)
    sent_all(*two)


def shards(source_features, target_features, conv_first, conv_second):
    n = lax.axis_size("tgt")
    rows, channels = source_features.shape
    local_rows, width = target_features.shape[:2]
    cells = rows * n
    hidden = conv_first.shape[0]
    assert local_rows == 2 and width == 128 and cells == 128 and hidden == 16
    padded_rows = -(-rows // 8) * 8
    if padded_rows != rows:
        source_features = jnp.pad(source_features, ((0, padded_rows - rows), (0, 0)))
    selectors = (jnp.asarray(first_selector(), BF16), jnp.asarray(second_selector(), BF16))
    operands = (
        source_features,
        target_features.reshape(local_rows * width, channels),
        jnp.transpose(conv_first, (1, 2, 3, 4, 0)).reshape(27, 3, hidden),
        jnp.transpose(conv_second, (1, 2, 3, 4, 0)).reshape(27, 3, hidden),
        *selectors,
    )
    dma = pltpu.SemaphoreType.DMA
    result = pl.pallas_call(
        functools.partial(kernel, n, rows, cells),
        out_shape=pltpu.VMEM((cells * local_rows, width), F32),
        in_specs=[pl.BlockSpec(memory_space=pl.ANY)] * len(operands),
        out_specs=pl.BlockSpec(memory_space=pltpu.VMEM),
        scratch_shapes=[
            *[pltpu.VMEM(operand.shape, operand.dtype) for operand in operands[1:]],
            pltpu.VMEM((2, 128, 128), F32),
            pltpu.VMEM((n, padded_rows, channels), BF16),
            pltpu.VMEM((local_rows * width, channels), BF16),
            pltpu.VMEM((local_rows, cells, width), F32),
            pltpu.VMEM((2, local_rows, cells, width), F32),
            pltpu.VMEM((n, 1, 128), F32),
            pltpu.VMEM((n, 1, 128), F32),
            pltpu.VMEM(((cells + 1) * SPAN, width), F32),
            pltpu.VMEM((cells + 8, 128), F32),
            pltpu.VMEM((cells + 2, COLUMN, width), BF16),
            pltpu.VMEM((STEPS, 2, 256, 256), BF16),
            pltpu.VMEM((STEPS, 2, 256, 256), BF16),
            pltpu.VMEM((cells * 2 + 8, width), F32),
            pltpu.VMEM((256, 256), BF16),
            pltpu.VMEM((96, 256), BF16),
            dma((len(operands),)), dma((n,)), dma((n,)), dma((n,)), dma((2, 2)), dma((2, 2)),
            dma((n,)), dma((n,)), dma((n,)), dma((n,)),
        ],
        compiler_params=pltpu.CompilerParams(
            collective_id=0, has_side_effects=True, vmem_limit_bytes=VMEM_BYTES
        ),
        cost_estimate=pl.CostEstimate(
            flops=2 * 10**9, bytes_accessed=3 * 10**6, transcendentals=0
        ),
    )(*operands)
    return result.reshape(1, cells, local_rows, width)


def solution(mesh):
    placed = (P(("pairs", "tgt"), None), P(("pairs", "tgt"), None, None), P(), P())
    return jax.shard_map(
        shards, mesh=mesh, in_specs=placed, out_specs=P("pairs", None, "tgt", None), check_vma=False
    )
```
